128 devices in a mesh: events: 4 (over y_lo, core), slab: 32 (over x, y_hi, z).
Axes of the slice: x: 4, y: 4 (y_hi: 2, y_lo: 2; y = y_hi * 2 + y_lo), z: 4, core: 2. Of those that a mesh axis runs over, the one named last changes fastest.
Arguments:
- partials: float32 [16, 3, 32768, 128], P('events', None, 'slab'), may hold values from -24 to 24
- coords: float32 [3, 32768, 128], P(None, 'slab'), may hold values from 0 to 1536, as said below
- neighbours: int32 [32768, 9], P('slab'), may hold values from -1 to 32767, as said below
- counts: int32 [32768], P('slab'), may hold values from 1 to 128
Outputs:
- smoothed: float32 [3, 32768, 128], P(None, 'slab', 'events')
The draws below stay inside these ranges and needn't reach their ends.
Inputs may be any that keep to these rules, and one draw needn't show every extreme that they name: `neighbours`: entry 0 of each row is the tile itself; the other entries are distinct tiles whose row (id // 256) and column (id % 256) each differ from the tile's by at most one, or -1 for an unused slot. `coords`: tile t's points have x in [6 r, 6 r + 6) with r = t // 256, y in [6 c, 6 c + 6) with c = t % 256, z in [0, 6).
All inputs are finite; a program needn't handle non-finite values.
Results may differ from the reference program's by a relative error of at most 0.0003.
Values sent between devices are 32-bit elements; how exact they have to be, the bound alone decides.
A program may use at most 64 MiB of HBM per device.

```python
import math
import jax
import jax.numpy as jnp
from jax import lax

P_SIZE = 128
NB = 9
FACE = 256
GROUPS = 16
TILES = 32768


def draw_neighbours(key, part):
    key = jax.random.fold_in(key, 11)
    key_order, key_live = jax.random.split(key)
    tile_ids = jnp.arange(TILES, dtype=jnp.int32)
    row_ids = tile_ids // FACE
    col_ids = tile_ids % FACE
    row_steps = jnp.array([-1, -1, -1, 0, 0, 1, 1, 1], jnp.int32)
    col_steps = jnp.array([-1, 0, 1, -1, 1, -1, 0, 1], jnp.int32)
    scores = jax.random.randint(key_order, (TILES, 8), 0, 1 << 20) * 8 + jnp.arange(8, dtype=jnp.int32)[None, :]
    order = jnp.argsort(scores, axis=1)
    rows_next = row_ids[:, None] + row_steps[order]
    cols_next = col_ids[:, None] + col_steps[order]
    keep = jax.random.randint(key_live, (TILES, 1), 4, 9)
    rank = jnp.arange(8, dtype=jnp.int32)[None, :]
    inside = (rows_next >= 0) & (rows_next < TILES // FACE) & (cols_next >= 0) & (cols_next < FACE) & (rank < keep)
    others = jnp.where(inside, rows_next * FACE + cols_next, -1)
    return jnp.concatenate([tile_ids[:, None], others], axis=1).astype(jnp.int32)


def draw_coords(key, part):
    key = jax.random.fold_in(key, 23)
    spread = jax.random.uniform(key, (3, TILES, P_SIZE), jnp.float32)
    tile_ids = jnp.arange(TILES, dtype=jnp.int32)
    rows = (tile_ids // FACE).astype(jnp.float32)[:, None]
    cols = (tile_ids % FACE).astype(jnp.float32)[:, None]
    coord_x = (rows + spread[0]) * 6.0
    coord_y = (cols + spread[1]) * 6.0
    coord_z = spread[2] * 6.0
    return jnp.stack([coord_x, coord_y, coord_z]).astype(jnp.float32)


def touch_ends(entries, rng, smallest, largest):
    longest = entries.shape.index(max(entries.shape))
    spots = []
    for shift in (0, 1):
        where = [jax.random.randint(jax.random.fold_in(rng, axis), (), 0, length) for axis, length in enumerate(entries.shape)]
        where[longest] = (where[longest] + shift) % entries.shape[longest]
        spots.append(tuple(where))
    return entries.at[spots[0]].set(smallest).at[spots[1]].set(largest)


def level_of(key, dims, cuts, least, top_value):
    def one(dim, shards_of):
        heights = jax.random.uniform(jax.random.fold_in(jax.random.fold_in(key, 6), dim), (shards_of,), jnp.float32, least / len(cuts), top_value / len(cuts))
        return jnp.repeat(jnp.exp(heights), dims[dim] // shards_of).reshape((-1,) + (1,) * (len(dims) - dim - 1))

    level = one(*cuts[0])
    for cut in cuts[1:]:
        level = level * one(*cut)
    return level


def normal_values(own_key, extent, scale, limit, pieces=(), kind=jnp.bfloat16):
    values = jax.random.normal(own_key, extent, jnp.float32) * scale
    if len(pieces) > 0:
        values = level_of(own_key, extent, pieces, -0.22, 0.18) * values
    return jnp.clip(values, min=-limit, max=limit).astype(kind)


def setup_inputs(seed: int = 0) -> dict:
    arg_keys = jax.random.split(jax.random.key(seed), 5)
    partials = normal_values(arg_keys[0], (GROUPS, 3, TILES, P_SIZE), 4.0, 24.0, ((0, 4), (2, 32)), jnp.float32)
    coords = draw_coords(jax.random.fold_in(arg_keys[4], 71), 0)
    neighbours = draw_neighbours(jax.random.fold_in(arg_keys[4], 71), 0)
    counts = touch_ends(jax.random.randint(arg_keys[3], (TILES,), 1, P_SIZE + 1), jax.random.fold_in(arg_keys[3], 1), 1, P_SIZE).astype(jnp.int32)
    return {"partials": partials, "coords": coords, "neighbours": neighbours, "counts": counts}


def weigh(queries, sources, used):
    diff_x = queries[0][:, :, None] - sources[0][:, None, :]
    diff_y = queries[1][:, :, None] - sources[1][:, None, :]
    diff_z = queries[2][:, :, None] - sources[2][:, None, :]
    spread = -(diff_x * diff_x + diff_y * diff_y) * (0.5 / 64.0) - diff_z * diff_z * (0.5 / 4.0)
    return jnp.exp(spread) * used[:, None, :]


def reference(partials, coords, neighbours, counts):
    total = jnp.sum(partials, axis=0)
    point_ids = lax.broadcasted_iota(jnp.int32, (TILES, P_SIZE), 1)
    valid = (point_ids < counts[:, None]).astype(jnp.float32)
    live = neighbours >= 0
    safe_ids = jnp.where(live, neighbours, 0).astype(jnp.int32)
    block = math.gcd(TILES, 64)

    def one(start):
        tile_ids = lax.dynamic_slice_in_dim(safe_ids, start, block, 0)
        slots_on = lax.dynamic_slice_in_dim(live, start, block, 0).astype(jnp.float32)
        queries = lax.dynamic_slice_in_dim(coords, start, block, 1)
        source_xyz = jnp.take(coords, tile_ids, axis=1).reshape(3, block, NB * P_SIZE)
        source_ker = jnp.take(total, tile_ids, axis=1).reshape(3, block, NB * P_SIZE)
        source_on = (jnp.take(valid, tile_ids, axis=0) * slots_on[:, :, None]).reshape(block, NB * P_SIZE)
        weight = weigh(queries, source_xyz, source_on)
        numer = jnp.einsum("bqs,kbs->kbq", weight, source_ker, precision=lax.Precision.HIGHEST)
        denom = jnp.sum(weight, axis=2)
        query_on = lax.dynamic_slice_in_dim(valid, start, block, 0) > 0.5
        return jnp.where(query_on[None], numer / jnp.where(query_on, denom, 1.0)[None], 0.0)

    starts = jnp.arange(TILES // block, dtype=jnp.int32) * block
    result = lax.map(one, starts)
    return jnp.transpose(result, (1, 0, 2, 3)).reshape(3, TILES, P_SIZE)
```

```python
import functools
import math

import jax
import jax.numpy as jnp
from jax import lax
from jax.experimental import pallas as pl
from jax.experimental.pallas import tpu as pltpu
from jax.sharding import PartitionSpec as P

MESH = pl.DeviceIdType.MESH
F32 = jnp.float32
BF16 = jnp.bfloat16

FACE = 256
ROWS = 4
PTS = 128
COLS = 64
WIN = 80
SLOTS = 9
SIDE = 6.0
CHUNK = 256
UNROLL = 16
NULL = (ROWS + 2) * FACE
LOG2E = math.log2(math.e)
SCALE_XY = math.sqrt(LOG2E / 128.0)
SCALE_Z = math.sqrt(LOG2E / 8.0)
ROW_ORDER = (0, 3, 1, 2)


def window(d):
    return pl.multiple_of(COLS * d - 8 + 8 * ((3 - d) // 3) - 8 * (d // 3), 8)


def place():
    return lax.axis_index("slab"), lax.axis_index("events")


def gather_kernel(
    slabs, parts, coords, counts, tot, xyz, cnt,
    pbuf, loc, rx1, tx2, rx2, psem, lsem, s1, r1, s2, r2, hs, hr,
):
    slab, me = place()
    high, core = me // 2, me % 2
    mate = 2 * high + (1 - core)
    across = 2 * (1 - high) + core

    loads = []
    for i, row in enumerate(ROW_ORDER):
        load = pltpu.make_async_copy(
            parts.at[:, :, pl.ds(row * FACE, FACE), :], pbuf.at[row], psem.at[row]
        )
        load.start()
        loads.append(load)
    mine = window(me)
    local = [pltpu.make_async_copy(counts, cnt.at[1], lsem.at[ROWS])]
    for row in range(ROWS):
        local.append(
            pltpu.make_async_copy(
                coords.at[:, pl.ds(row * FACE + mine, WIN), :], xyz.at[row + 1], lsem.at[row]
            )
        )
    for copy in local:
        copy.start()

    barrier = pltpu.get_barrier_semaphore()
    for other in (mate, across):
        pl.semaphore_signal(barrier, inc=1, device_id={"events": other}, device_id_type=MESH)

    @pl.when(slab > 0)
    def _():
        pl.semaphore_signal(barrier, inc=1, device_id={"slab": slab - 1}, device_id_type=MESH)

    @pl.when(slab < slabs - 1)
    def _():
        pl.semaphore_signal(barrier, inc=1, device_id={"slab": slab + 1}, device_id_type=MESH)

    pl.semaphore_wait(barrier, 4 - (slabs - 1 - slab) // (slabs - 1) - slab // (slabs - 1))

    def halo(up):
        target = slab - 1 if up else slab + 1
        row = 0 if up else ROWS - 1
        land = ROWS + 1 if up else 0
        side = 0 if up else 1
        pairs = (
            (coords.at[:, pl.ds(row * FACE + mine, WIN), :], xyz.at[land]),
            (counts, cnt.at[2 if up else 0]),
            (tot.at[row + 1], tot.at[land]),
        )
        return [
            pltpu.make_async_remote_copy(
                src_ref=src, dst_ref=dst, send_sem=hs.at[side, i], recv_sem=hr.at[side, i],
                device_id={"slab": target}, device_id_type=MESH,
            )
            for i, (src, dst) in enumerate(pairs)
        ]

    ups, downs = halo(True), halo(False)

    @pl.when(slab > 0)
    def _():
        ups[0].start()
        ups[1].start()

    @pl.when(slab < slabs - 1)
    def _():
        downs[0].start()
        downs[1].start()

    first = {}
    for i, row in enumerate(ROW_ORDER):
        loads[i].wait()
        loc[row] = (pbuf[row, 0] + pbuf[row, 1]) + (pbuf[row, 2] + pbuf[row, 3])
        for half in range(2):
            copy = pltpu.make_async_remote_copy(
                src_ref=loc.at[row, :, pl.ds(window(2 * half + 1 - core), WIN), :],
                dst_ref=rx1.at[row, half],
                send_sem=s1.at[row, half], recv_sem=r1.at[row, half],
                device_id={"events": mate}, device_id_type=MESH,
            )
            copy.start()
            first[row, half] = copy
    second = {}
    theirs = window(across)
    for row in ROW_ORDER:
        for half in range(2):
            first[row, half].wait_recv()
        tx2[row] = loc[row, :, pl.ds(theirs, WIN), :] + rx1[row, 1 - high]
        copy = pltpu.make_async_remote_copy(
            src_ref=tx2.at[row], dst_ref=rx2.at[row],
            send_sem=s2.at[row], recv_sem=r2.at[row],
            device_id={"events": across}, device_id_type=MESH,
        )
        copy.start()
        second[row] = copy
    for row in ROW_ORDER:
        second[row].wait_recv()
        tot[row + 1] = (loc[row, :, pl.ds(mine, WIN), :] + rx1[row, high]) + rx2[row]
        if row == 0:

            @pl.when(slab > 0)
            def _():
                ups[2].start()

        if row == ROWS - 1:

            @pl.when(slab < slabs - 1)
            def _():
                downs[2].start()

    for copy in local:
        copy.wait()
    for row in ROW_ORDER:
        for half in range(2):
            first[row, half].wait_send()
        second[row].wait_send()

    @pl.when(slab > 0)
    def _():
        for copy in ups:
            copy.wait_send()
        for copy in downs:
            copy.wait_recv()

    @pl.when(slab < slabs - 1)
    def _():
        for copy in downs:
            copy.wait_send()
        for copy in ups:
            copy.wait_recv()

    @pl.when(slab == 0)
    def _():
        tot[0] = jnp.zeros(tot.shape[1:], F32)
        xyz[0] = jnp.zeros(xyz.shape[1:], F32)
        cnt[0] = jnp.zeros(cnt.shape[1:], jnp.int32)

    @pl.when(slab == slabs - 1)
    def _():
        tot[ROWS + 1] = jnp.zeros(tot.shape[1:], F32)
        xyz[ROWS + 1] = jnp.zeros(xyz.shape[1:], F32)
        cnt[2] = jnp.zeros(cnt.shape[1:], jnp.int32)


def gather(slabs, partials, coords, counts):
    vmem = pl.BlockSpec(memory_space=pltpu.VMEM)
    hbm = pl.BlockSpec(memory_space=pl.ANY)
    dma = pltpu.SemaphoreType.DMA
    return pl.pallas_call(
        functools.partial(gather_kernel, slabs),
        out_shape=(
            jax.ShapeDtypeStruct((ROWS + 2, 3, WIN, PTS), F32),
            jax.ShapeDtypeStruct((ROWS + 2, 3, WIN, PTS), F32),
            jax.ShapeDtypeStruct((3, 8, PTS), jnp.int32),
        ),
        in_specs=[hbm, hbm, vmem],
        out_specs=(vmem, vmem, vmem),
        scratch_shapes=[
            pltpu.VMEM((ROWS, 4, 3, FACE, PTS), F32),
            pltpu.VMEM((ROWS, 3, FACE, PTS), F32),
            pltpu.VMEM((ROWS, 2, 3, WIN, PTS), F32),
            pltpu.VMEM((ROWS, 3, WIN, PTS), F32),
            pltpu.VMEM((ROWS, 3, WIN, PTS), F32),
            dma((ROWS,)), dma((ROWS + 1,)),
            dma((ROWS, 2)), dma((ROWS, 2)), dma((ROWS,)), dma((ROWS,)),
            dma((2, 3)), dma((2, 3)),
        ],
        compiler_params=pltpu.CompilerParams(
            collective_id=0, has_side_effects=True, vmem_limit_bytes=48 << 20
        ),
    )(partials, coords, counts)


def split(values):
    high = values.astype(BF16)
    return high, (values - high.astype(F32)).astype(BF16)


def smooth_kernel(place, tot, xyz, cnt, nbr, out, src, packed, acc, owner):
    slab, me = place()
    start = window(me)
    lane = lax.broadcasted_iota(jnp.int32, (8, PTS), 1)
    sub = lax.broadcasted_iota(jnp.int32, (8, PTS), 0)
    zero = jnp.zeros((8, PTS), F32)

    def build(step, _):
        row = step // (WIN // 8)
        col = pl.multiple_of(step % (WIN // 8) * 8, 8)
        tile = row * FACE + start + col
        limit = jnp.zeros((8, PTS), jnp.int32)
        for i in range(8):
            limit = jnp.where(sub == i, cnt[tile + i + (ROWS - 1) * FACE], limit)
        valid = lane < limit
        for i in range(3):
            src[pl.ds(tile * 8 + i, 8, 8), :] = jnp.where(valid, tot[row, i, pl.ds(col, 8), :], 0.0)
            src[pl.ds(tile * 8 + 4 + i, 8, 8), :] = jnp.where(valid, xyz[row, i, pl.ds(col, 8), :], 0.0)
        src[pl.ds(tile * 8 + 3, 8, 8), :] = valid.astype(F32)
        src[pl.ds(tile * 8 + 7, 8, 8), :] = zero
        return 0

    lax.fori_loop(0, (ROWS + 2) * (WIN // 8), build, 0)
    src[NULL * 8 : NULL * 8 + 8, :] = zero

    offset = slab * (ROWS * FACE) - FACE

    def pack(tile, base):
        own = tile // COLS * FACE + me * COLS + tile % COLS
        filled = 0
        current = zero
        for slot in range(SLOTS):
            entry = nbr[own * SLOTS + slot]
            live = entry >= 0
            which = jnp.where(live, entry - offset, NULL)
            used = jnp.where(live, cnt[jnp.where(live, which + (ROWS - 1) * FACE, 0)], 0)
            shift = filled % PTS
            turned = pltpu.roll(src[pl.ds(pl.multiple_of(which * 8, 8), 8), :], shift, 1)
            current = jnp.where(lane >= shift, turned, current)
            packed[base * 2 + filled // PTS] = current
            current = jnp.where(
                lane >= jnp.where(shift + used >= PTS, shift, PTS), 0.0,
                jnp.where(shift + used >= PTS, turned, current),
            )
            filled = filled + used
        packed[base * 2 + filled // PTS] = current
        packed[base * 2 + filled // PTS + 1] = zero
        for i in range((SLOTS * PTS + CHUNK - 1) // CHUNK):
            owner[base + i] = tile
        return base + (filled + CHUNK - 1) // CHUNK

    tiles = ROWS * COLS
    items = lax.fori_loop(0, tiles, pack, 0)

    def pad(i, _):
        owner[items + i] = tiles
        packed[(items + i) * 2] = zero
        packed[(items + i) * 2 + 1] = zero
        return 0

    lax.fori_loop(0, UNROLL, pad, 0)

    acc[...] = jnp.zeros_like(acc)
    scale = jnp.where(sub < 4, 1.0, jnp.where(sub < 6, SCALE_XY, SCALE_Z)).astype(F32)
    scale2 = jnp.where(sub < 4, 0.0, jnp.where(sub < 6, 2.0 * SCALE_XY, 2.0 * SCALE_Z)).astype(F32)
    minus = jnp.where((sub >= 4) & (sub < 7), -1.0, 0.0).astype(F32)
    minus = jnp.concatenate([minus, minus], axis=0).astype(BF16)

    def item(at):
        tile = owner[at]
        real = jnp.minimum(tile, tiles - 1)
        row, col = real // COLS, real % COLS + me * COLS
        centre_x = ((slab * ROWS + row).astype(F32) + 0.5) * SIDE
        centre_y = (col.astype(F32) + 0.5) * SIDE
        centre = jnp.where(
            sub < 4, 0.0, jnp.where(sub == 4, centre_x, jnp.where(sub == 5, centre_y, 0.5 * SIDE))
        )
        rest = jnp.concatenate([centre] * (CHUNK // PTS), axis=1)
        points = jnp.concatenate([packed[at * 2], packed[at * 2 + 1]], axis=1) - rest
        points = points * jnp.concatenate([scale] * (CHUNK // PTS), axis=1)
        high, low = split(points)
        both = jnp.concatenate([high, low], axis=0)
        sq_high, sq_low = split(points * points)
        sources = jnp.concatenate([both, both, sq_high, sq_low], axis=0)
        index = pl.multiple_of(((row + 1) * FACE + col) * 8, 8)
        query = (src[pl.ds(index, 8), :] - centre) * scale2
        q_high, q_low = split(query)
        queries = jnp.concatenate([q_high, q_high, q_low, q_low, minus], axis=0)
        return tile, both, sources, queries

    def work(step, _):
        todo = [item(step * UNROLL + i) for i in range(UNROLL)]
        spreads = [
            lax.dot_general(s, q, (((0,), (0,)), ((), ())), preferred_element_type=F32)
            for _, _, s, q in todo
        ]
        done = []
        for (tile, both, _, _), spread in zip(todo, spreads):
            high, low = split(jnp.exp2(spread))
            got = jnp.dot(both, jnp.concatenate([high, low], axis=1), preferred_element_type=F32)
            got = got[:, :PTS] + got[:, PTS:]
            done.append(got[:8] + got[8:])
        for (tile, _, _, _), got in zip(todo, done):
            at = pl.ds(pl.multiple_of(tile * 8, 8), 8)
            acc[at, :] = acc[at, :] + got
        return 0

    lax.fori_loop(0, (items + UNROLL - 1) // UNROLL, work, 0)

    def finish(step, _):
        row = step // 2
        half = step % 2
        quarters = []
        for part in range(4):
            tile = row * COLS + part * 16 + half * 8
            index = ((row + 1) * FACE + me * COLS + part * 16 + half * 8) * 8
            valid = src[pl.ds(index + 3, 8, 8), :] > 0.0
            below = jnp.where(valid, acc[pl.ds(tile * 8 + 3, 8, 8), :], 1.0)
            quarters.append(
                [jnp.where(valid, acc[pl.ds(tile * 8 + k, 8, 8), :] / below, 0.0) for k in range(3)]
            )
        for k in range(3):
            for d in range(4):
                value = zero
                for part in range(4):
                    turn = (part - d) * 32 % PTS
                    moved = pltpu.roll(quarters[part][k], turn, 1) if turn else quarters[part][k]
                    value = jnp.where(lane // 32 == part, moved, value)
                out[d, k, row, pl.ds(pl.multiple_of(half * 8, 8), 8), :] = value
        return 0

    lax.fori_loop(0, 2 * ROWS, finish, 0)


def smooth(place, tot, xyz, cnt, nbr):
    vmem = pl.BlockSpec(memory_space=pltpu.VMEM)
    smem = pl.BlockSpec(memory_space=pltpu.SMEM)
    tiles = ROWS * COLS
    most = tiles * ((SLOTS * PTS + CHUNK - 1) // CHUNK) + UNROLL
    return pl.pallas_call(
        functools.partial(smooth_kernel, place),
        out_shape=jax.ShapeDtypeStruct((4, 3, ROWS, 16, PTS), F32),
        in_specs=[vmem, vmem, smem, smem],
        out_specs=vmem,
        scratch_shapes=[
            pltpu.VMEM(((NULL + 1) * 8, PTS), F32),
            pltpu.VMEM((most * 2 + 8, 8, PTS), F32),
            pltpu.VMEM(((tiles + 1) * 8, PTS), F32),
            pltpu.SMEM((most + 8,), jnp.int32),
        ],
        compiler_params=pltpu.CompilerParams(vmem_limit_bytes=48 << 20),
    )(tot, xyz, cnt, nbr)


def share_kernel(mine, out, rx, ssem, rsem):
    slab, me = place()
    barrier = pltpu.get_barrier_semaphore()
    for i in range(1, 4):
        pl.semaphore_signal(barrier, inc=1, device_id={"events": (me + i) % 4}, device_id_type=MESH)
    pl.semaphore_wait(barrier, 3)
    copies = []
    for i in range(1, 4):
        target = (me + i) % 4
        copy = pltpu.make_async_remote_copy(
            src_ref=mine.at[target], dst_ref=rx.at[i - 1],
            send_sem=ssem.at[i - 1], recv_sem=rsem.at[i - 1],
            device_id={"events": target}, device_id_type=MESH,
        )
        copy.start()
        copies.append(copy)

    def unpack(block, load):
        for k in range(3):
            for row in range(ROWS):
                values = load(k, row)
                for part in range(4):
                    at = pl.multiple_of(row * FACE + block * COLS + part * 16, 16)
                    out[k, pl.ds(at, 16), :] = values[:, part * 32 : part * 32 + 32]

    unpack(me, lambda k, row: mine[me, k, row])
    for i in range(1, 4):
        copies[i - 1].wait_recv()
        unpack((me + 4 - i) % 4, lambda k, row: rx[i - 1, k, row])
    for copy in copies:
        copy.wait_send()


def share(mine):
    vmem = pl.BlockSpec(memory_space=pltpu.VMEM)
    dma = pltpu.SemaphoreType.DMA
    return pl.pallas_call(
        share_kernel,
        out_shape=jax.ShapeDtypeStruct((3, ROWS * FACE, 32), F32),
        in_specs=[vmem],
        out_specs=vmem,
        scratch_shapes=[pltpu.VMEM((3, 3, ROWS, 16, PTS), F32), dma((3,)), dma((3,))],
        compiler_params=pltpu.CompilerParams(
            collective_id=1, has_side_effects=True, vmem_limit_bytes=32 << 20
        ),
    )(mine)


def body(slabs, partials, coords, neighbours, counts):
    tot, xyz, cnt = gather(slabs, partials, coords, counts.reshape(8, PTS))
    mine = smooth(place, tot, xyz, cnt.reshape(-1), neighbours.reshape(-1))
    return share(mine)


def solution(mesh):
    placed = (P("events", None, "slab", None), P(None, "slab", None), P("slab", None), P("slab"))
    return jax.shard_map(
        functools.partial(body, mesh.shape["slab"]),
        mesh=mesh, in_specs=placed, out_specs=P(None, "slab", "events"), check_vma=False,
    )
```

```python
import functools
import math

import jax
import jax.numpy as jnp
from jax import lax
from jax.experimental import pallas as pl
from jax.experimental.pallas import tpu as pltpu
from jax.sharding import PartitionSpec as P

MESH = pl.DeviceIdType.MESH
F32 = jnp.float32
BF16 = jnp.bfloat16

FACE = 256
ROWS = 4
PTS = 128
COLS = 64
WIN = 80
SLOTS = 9
SIDE = 6.0
CHUNK = 256
UNROLL = 16
AHEAD = 8
MOST = (SLOTS * PTS + CHUNK - 1) // CHUNK
NULL = (ROWS + 2) * FACE
LOG2E = math.log2(math.e)
SCALE_XY = math.sqrt(LOG2E / 128.0)
SCALE_Z = math.sqrt(LOG2E / 8.0)
ROW_ORDER = (0, 3, 1, 2)


def window(d):
    return pl.multiple_of(COLS * d - 8 + 8 * ((3 - d) // 3) - 8 * (d // 3), 8)


def place():
    return lax.axis_index("slab"), lax.axis_index("events")


def gather_kernel(
    slabs, parts, coords, counts, tot, xyz, cnt,
    pbuf, loc, rx1, tx2, rx2, psem, lsem, s1, r1, s2, r2, hs, hr,
):
    slab, me = place()
    high, core = me // 2, me % 2
    mate = 2 * high + (1 - core)
    across = 2 * (1 - high) + core

    loads = []
    for i, row in enumerate(ROW_ORDER):
        load = pltpu.make_async_copy(
            parts.at[:, :, pl.ds(row * FACE, FACE), :], pbuf.at[row], psem.at[row]
        )
        load.start()
        loads.append(load)
    mine = window(me)
    local = [pltpu.make_async_copy(counts, cnt.at[1], lsem.at[ROWS])]
    for row in range(ROWS):
        local.append(
            pltpu.make_async_copy(
                coords.at[:, pl.ds(row * FACE + mine, WIN), :], xyz.at[row + 1], lsem.at[row]
            )
        )
    for copy in local:
        copy.start()

    barrier = pltpu.get_barrier_semaphore()
    for other in (mate, across):
        pl.semaphore_signal(barrier, inc=1, device_id={"events": other}, device_id_type=MESH)

    @pl.when(slab > 0)
    def _():
        pl.semaphore_signal(barrier, inc=1, device_id={"slab": slab - 1}, device_id_type=MESH)

    @pl.when(slab < slabs - 1)
    def _():
        pl.semaphore_signal(barrier, inc=1, device_id={"slab": slab + 1}, device_id_type=MESH)

    pl.semaphore_wait(barrier, 4 - (slabs - 1 - slab) // (slabs - 1) - slab // (slabs - 1))

    def halo(up):
        target = slab - 1 if up else slab + 1
        row = 0 if up else ROWS - 1
        land = ROWS + 1 if up else 0
        side = 0 if up else 1
        pairs = (
            (coords.at[:, pl.ds(row * FACE + mine, WIN), :], xyz.at[land]),
            (counts, cnt.at[2 if up else 0]),
            (tot.at[row + 1], tot.at[land]),
        )
        return [
            pltpu.make_async_remote_copy(
                src_ref=src, dst_ref=dst, send_sem=hs.at[side, i], recv_sem=hr.at[side, i],
                device_id={"slab": target}, device_id_type=MESH,
            )
            for i, (src, dst) in enumerate(pairs)
        ]

    ups, downs = halo(True), halo(False)

    @pl.when(slab > 0)
    def _():
        ups[0].start()
        ups[1].start()

    @pl.when(slab < slabs - 1)
    def _():
        downs[0].start()
        downs[1].start()

    first = {}
    for i, row in enumerate(ROW_ORDER):
        loads[i].wait()
        loc[row] = (pbuf[row, 0] + pbuf[row, 1]) + (pbuf[row, 2] + pbuf[row, 3])
        for half in range(2):
            copy = pltpu.make_async_remote_copy(
                src_ref=loc.at[row, :, pl.ds(window(2 * half + 1 - core), WIN), :],
                dst_ref=rx1.at[row, half],
                send_sem=s1.at[row, half], recv_sem=r1.at[row, half],
                device_id={"events": mate}, device_id_type=MESH,
            )
            copy.start()
            first[row, half] = copy
    second = {}
    theirs = window(across)
    for row in ROW_ORDER:
        for half in range(2):
            first[row, half].wait_recv()
        tx2[row] = loc[row, :, pl.ds(theirs, WIN), :] + rx1[row, 1 - high]
        copy = pltpu.make_async_remote_copy(
            src_ref=tx2.at[row], dst_ref=rx2.at[row],
            send_sem=s2.at[row], recv_sem=r2.at[row],
            device_id={"events": across}, device_id_type=MESH,
        )
        copy.start()
        second[row] = copy
    for row in ROW_ORDER:
        second[row].wait_recv()
        tot[row + 1] = (loc[row, :, pl.ds(mine, WIN), :] + rx1[row, high]) + rx2[row]
        if row == 0:

            @pl.when(slab > 0)
            def _():
                ups[2].start()

        if row == ROWS - 1:

            @pl.when(slab < slabs - 1)
            def _():
                downs[2].start()

    for copy in local:
        copy.wait()
    for row in ROW_ORDER:
        for half in range(2):
            first[row, half].wait_send()
        second[row].wait_send()

    @pl.when(slab > 0)
    def _():
        for copy in ups:
            copy.wait_send()
        for copy in downs:
            copy.wait_recv()

    @pl.when(slab < slabs - 1)
    def _():
        for copy in downs:
            copy.wait_send()
        for copy in ups:
            copy.wait_recv()

    @pl.when(slab == 0)
    def _():
        tot[0] = jnp.zeros(tot.shape[1:], F32)
        xyz[0] = jnp.zeros(xyz.shape[1:], F32)
        cnt[0] = jnp.zeros(cnt.shape[1:], jnp.int32)

    @pl.when(slab == slabs - 1)
    def _():
        tot[ROWS + 1] = jnp.zeros(tot.shape[1:], F32)
        xyz[ROWS + 1] = jnp.zeros(xyz.shape[1:], F32)
        cnt[2] = jnp.zeros(cnt.shape[1:], jnp.int32)


def gather(slabs, partials, coords, counts):
    vmem = pl.BlockSpec(memory_space=pltpu.VMEM)
    hbm = pl.BlockSpec(memory_space=pltpu.HBM)
    dma = pltpu.SemaphoreType.DMA
    return pl.pallas_call(
        functools.partial(gather_kernel, slabs),
        out_shape=(
            jax.ShapeDtypeStruct((ROWS + 2, 3, WIN, PTS), F32),
            jax.ShapeDtypeStruct((ROWS + 2, 3, WIN, PTS), F32),
            jax.ShapeDtypeStruct((3, 8, PTS), jnp.int32),
        ),
        in_specs=[hbm, hbm, hbm],
        out_specs=(vmem, vmem, vmem),
        scratch_shapes=[
            pltpu.VMEM((ROWS, 4, 3, FACE, PTS), F32),
            pltpu.VMEM((ROWS, 3, FACE, PTS), F32),
            pltpu.VMEM((ROWS, 2, 3, WIN, PTS), F32),
            pltpu.VMEM((ROWS, 3, WIN, PTS), F32),
            pltpu.VMEM((ROWS, 3, WIN, PTS), F32),
            dma((ROWS,)), dma((ROWS + 1,)),
            dma((ROWS, 2)), dma((ROWS, 2)), dma((ROWS,)), dma((ROWS,)),
            dma((2, 3)), dma((2, 3)),
        ],
        compiler_params=pltpu.CompilerParams(
            collective_id=0, has_side_effects=True, vmem_limit_bytes=52 << 20
        ),
    )(partials, coords, counts)


def split(values):
    high = values.astype(BF16)
    return high, (values - high.astype(F32)).astype(BF16)


def smooth_kernel(place, tot, xyz, cnt, nbr, out, src, packed, acc, spread, held, owner, before):
    slab, me = place()
    start = window(me)
    lane = lax.broadcasted_iota(jnp.int32, (8, PTS), 1)
    sub = lax.broadcasted_iota(jnp.int32, (8, PTS), 0)
    zero = jnp.zeros((8, PTS), F32)

    def build(step, _):
        row = step // (WIN // 8)
        col = pl.multiple_of(step % (WIN // 8) * 8, 8)
        tile = row * FACE + start + col
        limit = jnp.zeros((8, PTS), jnp.int32)
        for i in range(8):
            limit = jnp.where(sub == i, cnt[tile + i + (ROWS - 1) * FACE], limit)
        valid = lane < limit
        for i in range(3):
            src[pl.ds(tile * 8 + i, 8, 8), :] = jnp.where(valid, tot[row, i, pl.ds(col, 8), :], 0.0)
            src[pl.ds(tile * 8 + 4 + i, 8, 8), :] = jnp.where(valid, xyz[row, i, pl.ds(col, 8), :], 0.0)
        src[pl.ds(tile * 8 + 3, 8, 8), :] = valid.astype(F32)
        src[pl.ds(tile * 8 + 7, 8, 8), :] = zero
        return 0

    lax.fori_loop(0, (ROWS + 2) * (WIN // 8), build, 0)
    src[NULL * 8 : NULL * 8 + 8, :] = zero

    offset = slab * (ROWS * FACE) - FACE

    tiles = ROWS * COLS
    spare = tiles * MOST

    def pack(tile, base):
        own = (tile >> 6) * FACE + me * COLS + (tile & 63)
        filled = 0
        current = zero
        for slot in range(SLOTS):
            entry = nbr[slot, own]
            live = entry >= 0
            which = jnp.where(live, entry - offset, NULL)
            used = jnp.where(live, cnt[jnp.where(live, which + (ROWS - 1) * FACE, 0)], 0)
            shift = filled & 127
            turned = pltpu.roll(src[pl.ds(pl.multiple_of(which * 8, 8), 8), :], shift, 1)
            current = jnp.where(lane >= shift, turned, current)
            packed[base * 2 + (filled >> 7)] = current
            full = shift + used >= PTS
            current = jnp.where(
                lane >= jnp.where(full, shift, PTS), 0.0, jnp.where(full, turned, current)
            )
            filled = filled + used
        packed[base * 2 + (filled >> 7)] = current
        packed[base * 2 + (filled >> 7) + 1] = zero
        for i in range(MOST):
            owner[base + i] = tile
        return base + ((filled + CHUNK - 1) >> 8)

    packed[spare * 2] = zero
    packed[spare * 2 + 1] = zero
    owner[spare] = tiles
    acc[...] = jnp.zeros_like(acc)
    scale = jnp.where(sub < 4, 1.0, jnp.where(sub < 6, SCALE_XY, SCALE_Z)).astype(F32)
    scale2 = jnp.where(sub < 4, 0.0, jnp.where(sub < 6, 2.0 * SCALE_XY, 2.0 * SCALE_Z)).astype(F32)
    minus = jnp.where((sub >= 4) & (sub < 7), -1.0, 0.0).astype(F32)
    minus = jnp.concatenate([minus, minus], axis=0).astype(BF16)

    def item(at):
        tile = owner[at]
        real = jnp.minimum(tile, tiles - 1)
        row, col = real >> 6, (real & 63) + me * COLS
        centre_x = ((slab * ROWS + row).astype(F32) + 0.5) * SIDE
        centre_y = (col.astype(F32) + 0.5) * SIDE
        centre = jnp.where(
            sub < 4, 0.0, jnp.where(sub == 4, centre_x, jnp.where(sub == 5, centre_y, 0.5 * SIDE))
        )
        boths, squares = [], []
        for half in range(CHUNK // PTS):
            points = (packed[at * 2 + half] - centre) * scale
            boths.append(jnp.concatenate(split(points), axis=0))
            squares.append(jnp.concatenate(split(points * points), axis=0))
        both = jnp.concatenate(boths, axis=1)
        sources = jnp.concatenate([both, both, jnp.concatenate(squares, axis=1)], axis=0)
        index = pl.multiple_of(((row + 1) * FACE + col) * 8, 8)
        query = (src[pl.ds(index, 8), :] - centre) * scale2
        q_high, q_low = split(query)
        queries = jnp.concatenate([q_high, q_high, q_low, q_low, minus], axis=0)
        return tile, both, sources, queries

    def advance(taken, made):
        todo = []
        for i in range(UNROLL):
            todo.append(item(jnp.where(taken + i < made, taken + i, spare)))
        for i, (tile, both, sources, queries) in enumerate(todo):
            high, low = split(jnp.exp2(spread[i]))
            got = jnp.dot(held[i], jnp.concatenate([high, low], axis=1), preferred_element_type=F32)
            got = got[:, :PTS] + got[:, PTS:]
            at = pl.ds(pl.multiple_of(before[i] * 8, 8), 8)
            acc[at, :] = acc[at, :] + (got[:8] + got[8:])
            spread[i] = lax.dot_general(
                sources, queries, (((0,), (0,)), ((), ())), preferred_element_type=F32
            )
            held[i] = both
            before[i] = tile
        return jnp.minimum(taken + UNROLL, made)

    for i in range(UNROLL):
        before[i] = tiles

    def fused(step, carry):
        made, taken = carry
        taken = advance(taken, made)
        for i in range(AHEAD):
            made = pack(step * AHEAD + i, made)
        return made, taken

    made, taken = lax.fori_loop(0, tiles // AHEAD, fused, (0, 0))
    lax.fori_loop(0, (made - taken + UNROLL - 1) // UNROLL + 1, lambda _, t: advance(t, made), taken)

    for pair in range(ROWS // 2):
        top = pair * 2 * COLS * 8
        flags = [
            src[pl.ds(((2 * pair + i + 1) * FACE + me * COLS) * 8 + 3, COLS, 8), :] for i in range(2)
        ]
        valid = jnp.concatenate(flags, axis=0) > 0.0
        share = 1.0 / jnp.where(valid, acc[pl.ds(top + 3, 2 * COLS, 8), :], 1.0)
        for k in range(3):
            value = jnp.where(valid, acc[pl.ds(top + k, 2 * COLS, 8), :] * share, 0.0).T
            for d in range(4):
                out[d, k, pair] = value[d * 32 : d * 32 + 32]


def smooth(place, tot, xyz, cnt, nbr):
    vmem = pl.BlockSpec(memory_space=pltpu.VMEM)
    smem = pl.BlockSpec(memory_space=pltpu.SMEM)
    tiles = ROWS * COLS
    most = tiles * MOST + 1
    return pl.pallas_call(
        functools.partial(smooth_kernel, place),
        out_shape=jax.ShapeDtypeStruct((4, 3, ROWS // 2, 32, PTS), F32),
        in_specs=[vmem, vmem, smem, smem],
        out_specs=vmem,
        scratch_shapes=[
            pltpu.VMEM(((NULL + 1) * 8, PTS), F32),
            pltpu.VMEM((most * 2, 8, PTS), F32),
            pltpu.VMEM(((tiles + 1) * 8, PTS), F32),
            pltpu.VMEM((UNROLL, CHUNK, PTS), F32),
            pltpu.VMEM((UNROLL, 16, CHUNK), BF16),
            pltpu.SMEM((most + 8,), jnp.int32),
            pltpu.SMEM((UNROLL,), jnp.int32),
        ],
        compiler_params=pltpu.CompilerParams(vmem_limit_bytes=48 << 20),
    )(tot, xyz, cnt, nbr)


def share_kernel(mine, out, rx, ssem, rsem):
    slab, me = place()
    barrier = pltpu.get_barrier_semaphore()
    for i in range(1, 4):
        pl.semaphore_signal(barrier, inc=1, device_id={"events": (me + i) % 4}, device_id_type=MESH)
    pl.semaphore_wait(barrier, 3)

    def copy(target, slot):
        return pltpu.make_async_remote_copy(
            src_ref=mine.at[target], dst_ref=rx.at[slot],
            send_sem=ssem.at[target], recv_sem=rsem.at[slot],
            device_id={"events": target}, device_id_type=MESH,
        )

    for i in (2, 3, 1):
        copy((me + i) % 4, me).start()
    rx[me] = mine[me]
    for i in (1, 3, 2):
        other = (me + i) % 4
        copy(other, other).wait_recv()
    left = lax.broadcasted_iota(jnp.int32, (32, PTS), 1) < COLS
    for k in range(3):
        for pair in range(ROWS // 2):
            for half in range(2):
                a, b = rx[2 * half, k, pair], rx[2 * half + 1, k, pair]
                upper = 2 * pair * FACE + half * PTS
                lower = upper + FACE
                out[k, :, upper : upper + PTS] = jnp.where(left, a, pltpu.roll(b, COLS, 1))
                out[k, :, lower : lower + PTS] = jnp.where(left, pltpu.roll(a, COLS, 1), b)
    for i in range(1, 4):
        copy((me + i) % 4, me).wait_send()


def share(mine):
    vmem = pl.BlockSpec(memory_space=pltpu.VMEM)
    dma = pltpu.SemaphoreType.DMA
    return pl.pallas_call(
        share_kernel,
        out_shape=jax.ShapeDtypeStruct((3, 32, ROWS * FACE), F32),
        in_specs=[vmem],
        out_specs=vmem,
        scratch_shapes=[pltpu.VMEM((4, 3, ROWS // 2, 32, PTS), F32), dma((4,)), dma((4,))],
        compiler_params=pltpu.CompilerParams(
            collective_id=1, has_side_effects=True, vmem_limit_bytes=32 << 20
        ),
    )(mine)


def body(slabs, partials, coords, neighbours, counts):
    tot, xyz, cnt = gather(slabs, partials, coords, counts.reshape(8, PTS))
    mine = smooth(place, tot, xyz, cnt.reshape(-1), neighbours.T)
    return jnp.transpose(share(mine), (0, 2, 1))


def solution(mesh):
    placed = (P("events", None, "slab", None), P(None, "slab", None), P("slab", None), P("slab"))
    return jax.shard_map(
        functools.partial(body, mesh.shape["slab"]),
        mesh=mesh, in_specs=placed, out_specs=P(None, "slab", "events"), check_vma=False,
    )
```

```python
import functools
import math

import jax
import jax.numpy as jnp
from jax import lax
from jax.experimental import pallas as pl
from jax.experimental.pallas import tpu as pltpu
from jax.sharding import PartitionSpec as P

MESH = pl.DeviceIdType.MESH
F32 = jnp.float32
BF16 = jnp.bfloat16

FACE = 256
ROWS = 4
PTS = 128
COLS = 64
WIN = 80
SLOTS = 9
SIDE = 6.0
CHUNK = 256
UNROLL = 16
AHEAD = 8
MOST = (SLOTS * PTS + CHUNK - 1) // CHUNK
NULL = (ROWS + 2) * FACE
LOG2E = math.log2(math.e)
SCALE_XY = math.sqrt(LOG2E / 128.0)
SCALE_Z = math.sqrt(LOG2E / 8.0)
ROW_ORDER = (0, 3, 1, 2)


def window(d):
    return pl.multiple_of(COLS * d - 8 + 8 * ((3 - d) // 3) - 8 * (d // 3), 8)


def swap(slab, index):
    return 2 * ((index // 2 + slab // 4) % 2) + index % 2


def place():
    slab = lax.axis_index("slab")
    return slab, swap(slab, lax.axis_index("events"))


def list_slots(slab, me, cnt, nbuf, table):
    lane = lax.broadcasted_iota(jnp.int32, (1, FACE), 1)
    near = []
    for row in range(-1, ROWS + 1):
        which, at = (row + ROWS) // ROWS, (row + ROWS) % ROWS * 2
        line = jnp.concatenate([cnt[which, at : at + 1, :], cnt[which, at + 1 : at + 2, :]], axis=1)
        wide = jnp.broadcast_to(line, (8, FACE))
        near.append([pltpu.roll(wide, 1, 1)[:1], line, pltpu.roll(wide, FACE - 1, 1)[:1]])
    second_half = jnp.broadcast_to(me // 2, (SLOTS, PTS)) == 1
    odd = jnp.broadcast_to(me % 2, (SLOTS, PTS)) == 1
    left = lax.broadcasted_iota(jnp.int32, (SLOTS, PTS), 1) < COLS

    def own(upper, lower):
        upper = jnp.where(second_half, upper[:, PTS:], upper[:, :PTS])
        lower = jnp.where(second_half, lower[:, PTS:], lower[:, :PTS])
        upper = jnp.where(odd, pltpu.roll(upper, COLS, 1), upper)
        lower = jnp.where(odd, lower, pltpu.roll(lower, COLS, 1))
        return jnp.where(left, upper, lower)

    sources, sizes = [], []
    for row in range(ROWS):
        entry = nbuf[:, row * FACE : (row + 1) * FACE]
        step = entry - (slab * (ROWS * FACE) + row * FACE + lane)
        used = jnp.zeros((SLOTS, FACE), jnp.int32)
        for i in range(3):
            for j in range(3):
                used = jnp.where(step == (i - 1) * FACE + j - 1, near[row + i][j], used)
        sizes.append(jnp.where(entry >= 0, used, 0))
        sources.append(jnp.where(entry >= 0, entry - (slab * (ROWS * FACE) - FACE), NULL))
    which = jnp.concatenate([own(*sources[:2]), own(*sources[2:])], axis=1)
    used = jnp.concatenate([own(*sizes[:2]), own(*sizes[2:])], axis=1)
    table[0:SLOTS, :] = which
    starts = [jnp.zeros((1, FACE), jnp.int32)]
    for slot in range(SLOTS):
        starts.append(starts[-1] + used[slot : slot + 1, :])
    chunks = jnp.broadcast_to((starts[-1] + (CHUNK - 1)) // CHUNK, (8, FACE))
    lanes = lax.broadcasted_iota(jnp.int32, (8, FACE), 1)
    ends = chunks
    for step in (1, 2, 4, 8, 16, 32, 64, 128):
        ends = ends + jnp.where(lanes >= step, pltpu.roll(ends, step, 1), 0)
    base = (ends - chunks)[:1] * CHUNK
    for slot in range(SLOTS + 1):
        table[SLOTS + slot : SLOTS + slot + 1, :] = base + starts[slot]


def gather_kernel(
    slabs, parts, coords, counts, nbr, tot, xyz, cnt, table,
    nbuf, pbuf, loc, rx1, tx2, rx2, psem, lsem, s1, r1, s2, r2, hs, hr,
):
    slab, me = place()
    high, core = me // 2, me % 2
    event = lax.axis_index("events")
    mate = 2 * (event // 2) + (1 - core)
    across = 2 * (1 - event // 2) + core

    loads = []
    for i, row in enumerate(ROW_ORDER):
        load = pltpu.make_async_copy(
            parts.at[:, :, pl.ds(row * FACE, FACE), :], pbuf.at[row], psem.at[row]
        )
        load.start()
        loads.append(load)
    mine = window(me)
    local = [
        pltpu.make_async_copy(counts, cnt.at[1], lsem.at[ROWS]),
        pltpu.make_async_copy(nbr, nbuf, lsem.at[ROWS + 1]),
    ]
    for row in range(ROWS):
        local.append(
            pltpu.make_async_copy(
                coords.at[:, pl.ds(row * FACE + mine, WIN), :], xyz.at[row + 1], lsem.at[row]
            )
        )
    for copy in local:
        copy.start()

    def beside(step):
        return {"slab": slab + step, "events": swap(slab + step, me)}

    barrier = pltpu.get_barrier_semaphore()
    for other in (mate, across):
        pl.semaphore_signal(barrier, inc=1, device_id={"events": other}, device_id_type=MESH)

    @pl.when(slab > 0)
    def _():
        pl.semaphore_signal(barrier, inc=1, device_id=beside(-1), device_id_type=MESH)

    @pl.when(slab < slabs - 1)
    def _():
        pl.semaphore_signal(barrier, inc=1, device_id=beside(1), device_id_type=MESH)

    pl.semaphore_wait(barrier, 4 - (slabs - 1 - slab) // (slabs - 1) - slab // (slabs - 1))

    def halo(up):
        row = 0 if up else ROWS - 1
        land = ROWS + 1 if up else 0
        side = 0 if up else 1
        pairs = (
            (coords.at[:, pl.ds(row * FACE + mine, WIN), :], xyz.at[land]),
            (counts, cnt.at[2 if up else 0]),
            (tot.at[row + 1], tot.at[land]),
        )
        return [
            pltpu.make_async_remote_copy(
                src_ref=src, dst_ref=dst, send_sem=hs.at[side, i], recv_sem=hr.at[side, i],
                device_id=beside(-1 if up else 1), device_id_type=MESH,
            )
            for i, (src, dst) in enumerate(pairs)
        ]

    ups, downs = halo(True), halo(False)

    @pl.when(slab > 0)
    def _():
        ups[0].start()
        ups[1].start()

    @pl.when(slab < slabs - 1)
    def _():
        downs[0].start()
        downs[1].start()

    first = {}
    for i, row in enumerate(ROW_ORDER):
        loads[i].wait()
        loc[row] = (pbuf[row, 0] + pbuf[row, 1]) + (pbuf[row, 2] + pbuf[row, 3])
        for half in range(2):
            copy = pltpu.make_async_remote_copy(
                src_ref=loc.at[row, :, pl.ds(window(2 * half + 1 - core), WIN), :],
                dst_ref=rx1.at[row, half],
                send_sem=s1.at[row, half], recv_sem=r1.at[row, half],
                device_id={"events": mate}, device_id_type=MESH,
            )
            copy.start()
            first[row, half] = copy
    for copy in local:
        copy.wait()

    @pl.when(slab > 0)
    def _():
        downs[1].wait_recv()

    @pl.when(slab < slabs - 1)
    def _():
        ups[1].wait_recv()

    @pl.when(slab == 0)
    def _():
        cnt[0] = jnp.zeros(cnt.shape[1:], jnp.int32)

    @pl.when(slab == slabs - 1)
    def _():
        cnt[2] = jnp.zeros(cnt.shape[1:], jnp.int32)

    second = {}
    theirs = window(2 * (1 - high) + core)
    for row in ROW_ORDER:
        for half in range(2):
            first[row, half].wait_recv()
        tx2[row] = loc[row, :, pl.ds(theirs, WIN), :] + rx1[row, 1 - high]
        copy = pltpu.make_async_remote_copy(
            src_ref=tx2.at[row], dst_ref=rx2.at[row],
            send_sem=s2.at[row], recv_sem=r2.at[row],
            device_id={"events": across}, device_id_type=MESH,
        )
        copy.start()
        second[row] = copy
    list_slots(slab, me, cnt, nbuf, table)
    for row in ROW_ORDER:
        second[row].wait_recv()
        tot[row + 1] = (loc[row, :, pl.ds(mine, WIN), :] + rx1[row, high]) + rx2[row]
        if row == 0:

            @pl.when(slab > 0)
            def _():
                ups[2].start()

        if row == ROWS - 1:

            @pl.when(slab < slabs - 1)
            def _():
                downs[2].start()

    for row in ROW_ORDER:
        for half in range(2):
            first[row, half].wait_send()
        second[row].wait_send()

    @pl.when(slab > 0)
    def _():
        for copy in ups:
            copy.wait_send()
        downs[0].wait_recv()
        downs[2].wait_recv()

    @pl.when(slab < slabs - 1)
    def _():
        for copy in downs:
            copy.wait_send()
        ups[0].wait_recv()
        ups[2].wait_recv()

    @pl.when(slab == 0)
    def _():
        tot[0] = jnp.zeros(tot.shape[1:], F32)
        xyz[0] = jnp.zeros(xyz.shape[1:], F32)

    @pl.when(slab == slabs - 1)
    def _():
        tot[ROWS + 1] = jnp.zeros(tot.shape[1:], F32)
        xyz[ROWS + 1] = jnp.zeros(xyz.shape[1:], F32)


def gather(slabs, partials, coords, counts, neighbours):
    vmem = pl.BlockSpec(memory_space=pltpu.VMEM)
    hbm = pl.BlockSpec(memory_space=pltpu.HBM)
    dma = pltpu.SemaphoreType.DMA
    return pl.pallas_call(
        functools.partial(gather_kernel, slabs),
        out_shape=(
            jax.ShapeDtypeStruct((ROWS + 2, 3, WIN, PTS), F32),
            jax.ShapeDtypeStruct((ROWS + 2, 3, WIN, PTS), F32),
            jax.ShapeDtypeStruct((3, 8, PTS), jnp.int32),
            jax.ShapeDtypeStruct((2 * SLOTS + 1, FACE), jnp.int32),
        ),
        in_specs=[hbm, hbm, hbm, hbm],
        out_specs=(vmem, vmem, vmem, vmem),
        scratch_shapes=[
            pltpu.VMEM((SLOTS, ROWS * FACE), jnp.int32),
            pltpu.VMEM((ROWS, 4, 3, FACE, PTS), F32),
            pltpu.VMEM((ROWS, 3, FACE, PTS), F32),
            pltpu.VMEM((ROWS, 2, 3, WIN, PTS), F32),
            pltpu.VMEM((ROWS, 3, WIN, PTS), F32),
            pltpu.VMEM((ROWS, 3, WIN, PTS), F32),
            dma((ROWS,)), dma((ROWS + 2,)),
            dma((ROWS, 2)), dma((ROWS, 2)), dma((ROWS,)), dma((ROWS,)),
            dma((2, 3)), dma((2, 3)),
        ],
        compiler_params=pltpu.CompilerParams(
            collective_id=0, has_side_effects=True, vmem_limit_bytes=52 << 20
        ),
    )(partials, coords, counts, neighbours)


def split(values):
    high = values.astype(BF16)
    return high, (values - high.astype(F32)).astype(BF16)


def smooth_kernel(place, tot, xyz, cnt, table, out, src, packed, acc, spread, held, owner, before):
    slab, me = place()
    start = window(me)
    lane = lax.broadcasted_iota(jnp.int32, (8, PTS), 1)
    sub = lax.broadcasted_iota(jnp.int32, (8, PTS), 0)
    zero = jnp.zeros((8, PTS), F32)

    def build(step, _):
        row = step // (WIN // 8)
        col = pl.multiple_of(step % (WIN // 8) * 8, 8)
        tile = row * FACE + start + col
        limit = jnp.zeros((8, PTS), jnp.int32)
        for i in range(8):
            limit = jnp.where(sub == i, cnt[tile + i + (ROWS - 1) * FACE], limit)
        valid = lane < limit
        for i in range(3):
            src[pl.ds(tile * 8 + i, 8, 8), :] = jnp.where(valid, tot[row, i, pl.ds(col, 8), :], 0.0)
            src[pl.ds(tile * 8 + 4 + i, 8, 8), :] = jnp.where(valid, xyz[row, i, pl.ds(col, 8), :], 0.0)
        src[pl.ds(tile * 8 + 3, 8, 8), :] = valid.astype(F32)
        src[pl.ds(tile * 8 + 7, 8, 8), :] = zero
        return 0

    lax.fori_loop(0, (ROWS + 2) * (WIN // 8), build, 0)
    src[NULL * 8 : NULL * 8 + 8, :] = zero

    tiles = ROWS * COLS
    spare = tiles * MOST

    def pack(tile):
        for slot in range(SLOTS):
            which, at = table[slot, tile], table[SLOTS + slot, tile]
            shift, index = at & (PTS - 1), at >> 7
            turned = pltpu.roll(src[pl.ds(pl.multiple_of(which * 8, 8), 8), :], shift, 1)
            here = lane >= shift
            pltpu.store(packed.at[index], turned, mask=here)
            pltpu.store(packed.at[index + 1], turned, mask=jnp.logical_not(here))
        end = table[2 * SLOTS, tile]
        pltpu.store(packed.at[end >> 7], zero, mask=lane >= (end & (PTS - 1)))
        packed[(end >> 7) + 1] = zero
        first = table[SLOTS, tile] >> 8
        for i in range(MOST):
            owner[first + i] = tile

    packed[spare * 2] = zero
    packed[spare * 2 + 1] = zero
    owner[spare] = tiles
    acc[...] = jnp.zeros_like(acc)
    scale = jnp.where(sub < 4, 1.0, jnp.where(sub < 6, SCALE_XY, SCALE_Z)).astype(F32)
    scale2 = jnp.where(sub < 4, 0.0, jnp.where(sub < 6, 2.0 * SCALE_XY, 2.0 * SCALE_Z)).astype(F32)
    minus = jnp.where((sub >= 4) & (sub < 7), -1.0, 0.0).astype(F32)
    minus = jnp.concatenate([minus, minus], axis=0).astype(BF16)

    def item(at):
        tile = owner[at]
        row, col = tile >> 6, (tile & 63) + me * COLS
        centre_x = ((slab * ROWS + row).astype(F32) + 0.5) * SIDE
        centre_y = (col.astype(F32) + 0.5) * SIDE
        centre = jnp.where(
            sub < 4, 0.0, jnp.where(sub == 4, centre_x, jnp.where(sub == 5, centre_y, 0.5 * SIDE))
        )
        boths, squares = [], []
        for half in range(CHUNK // PTS):
            points = (packed[at * 2 + half] - centre) * scale
            boths.append(jnp.concatenate(split(points), axis=0))
            squares.append(jnp.concatenate(split(points * points), axis=0))
        both = jnp.concatenate(boths, axis=1)
        sources = jnp.concatenate([both, both, jnp.concatenate(squares, axis=1)], axis=0)
        index = pl.multiple_of(((row + 1) * FACE + col) * 8, 8)
        query = (src[pl.ds(index, 8), :] - centre) * scale2
        q_high, q_low = split(query)
        queries = jnp.concatenate([q_high, q_high, q_low, q_low, minus], axis=0)
        return tile, both, sources, queries

    def advance(taken, made):
        todo = []
        for i in range(UNROLL):
            todo.append(item(jnp.where(taken + i < made, taken + i, spare)))
        for i, (tile, both, sources, queries) in enumerate(todo):
            high, low = split(jnp.exp2(spread[i]))
            got = jnp.dot(held[i], jnp.concatenate([high, low], axis=1), preferred_element_type=F32)
            got = got[:, :PTS] + got[:, PTS:]
            at = pl.ds(pl.multiple_of(before[i] * 8, 8), 8)
            acc[at, :] = acc[at, :] + (got[:8] + got[8:])
            spread[i] = lax.dot_general(
                sources, queries, (((0,), (0,)), ((), ())), preferred_element_type=F32
            )
            held[i] = both
            before[i] = tile
        return jnp.minimum(taken + UNROLL, made)

    for i in range(UNROLL):
        before[i] = tiles

    def fused(step, carry):
        made, taken = carry
        taken = advance(taken, made)
        for i in range(AHEAD):
            pack(step * AHEAD + i)
        return (table[2 * SLOTS, (step + 1) * AHEAD - 1] + (CHUNK - 1)) >> 8, taken

    made, taken = lax.fori_loop(0, tiles // AHEAD, fused, (0, 0))
    lax.fori_loop(0, (made - taken + UNROLL - 1) // UNROLL + 1, lambda _, t: advance(t, made), taken)

    for pair in range(ROWS // 2):
        top = pair * 2 * COLS * 8
        flags = [
            src[pl.ds(((2 * pair + i + 1) * FACE + me * COLS) * 8 + 3, COLS, 8), :] for i in range(2)
        ]
        valid = jnp.concatenate(flags, axis=0) > 0.0
        share = 1.0 / jnp.where(valid, acc[pl.ds(top + 3, 2 * COLS, 8), :], 1.0)
        for k in range(3):
            value = jnp.where(valid, acc[pl.ds(top + k, 2 * COLS, 8), :] * share, 0.0).T
            for d in range(4):
                out[d, k, pair] = value[d * 32 : d * 32 + 32]


def smooth(place, tot, xyz, cnt, table):
    vmem = pl.BlockSpec(memory_space=pltpu.VMEM)
    smem = pl.BlockSpec(memory_space=pltpu.SMEM)
    tiles = ROWS * COLS
    most = tiles * MOST + 1
    return pl.pallas_call(
        functools.partial(smooth_kernel, place),
        out_shape=jax.ShapeDtypeStruct((4, 3, ROWS // 2, 32, PTS), F32),
        in_specs=[vmem, vmem, smem, smem],
        out_specs=vmem,
        scratch_shapes=[
            pltpu.VMEM(((NULL + 1) * 8, PTS), F32),
            pltpu.VMEM((most * 2, 8, PTS), F32),
            pltpu.VMEM(((tiles + 1) * 8, PTS), F32),
            pltpu.VMEM((UNROLL, CHUNK, PTS), F32),
            pltpu.VMEM((UNROLL, 16, CHUNK), BF16),
            pltpu.SMEM((most + 8,), jnp.int32),
            pltpu.SMEM((UNROLL,), jnp.int32),
        ],
        compiler_params=pltpu.CompilerParams(vmem_limit_bytes=48 << 20),
    )(tot, xyz, cnt, table)


def share_kernel(mine, out, rx, ssem, rsem):
    slab, block = place()
    me = lax.axis_index("events")
    barrier = pltpu.get_barrier_semaphore()
    for i in range(1, 4):
        pl.semaphore_signal(barrier, inc=1, device_id={"events": (me + i) % 4}, device_id_type=MESH)
    pl.semaphore_wait(barrier, 3)

    def copy(target, slot):
        return pltpu.make_async_remote_copy(
            src_ref=mine.at[target], dst_ref=rx.at[slot],
            send_sem=ssem.at[target], recv_sem=rsem.at[slot],
            device_id={"events": target}, device_id_type=MESH,
        )

    for i in (2, 3, 1):
        copy((me + i) % 4, block).start()
    rx[block] = mine[me]
    for i in (1, 3, 2):
        other = (me + i) % 4
        copy(other, swap(slab, other)).wait_recv()
    left = lax.broadcasted_iota(jnp.int32, (32, PTS), 1) < COLS
    for k in range(3):
        for pair in range(ROWS // 2):
            for half in range(2):
                a, b = rx[2 * half, k, pair], rx[2 * half + 1, k, pair]
                upper = 2 * pair * FACE + half * PTS
                lower = upper + FACE
                out[k, :, upper : upper + PTS] = jnp.where(left, a, pltpu.roll(b, COLS, 1))
                out[k, :, lower : lower + PTS] = jnp.where(left, pltpu.roll(a, COLS, 1), b)
    for i in range(1, 4):
        copy((me + i) % 4, block).wait_send()


def share(mine):
    vmem = pl.BlockSpec(memory_space=pltpu.VMEM)
    dma = pltpu.SemaphoreType.DMA
    return pl.pallas_call(
        share_kernel,
        out_shape=jax.ShapeDtypeStruct((3, 32, ROWS * FACE), F32),
        in_specs=[vmem],
        out_specs=vmem,
        scratch_shapes=[pltpu.VMEM((4, 3, ROWS // 2, 32, PTS), F32), dma((4,)), dma((4,))],
        compiler_params=pltpu.CompilerParams(
            collective_id=1, has_side_effects=True, vmem_limit_bytes=32 << 20
        ),
    )(mine)


def body(slabs, partials, coords, neighbours, counts):
    tot, xyz, cnt, table = gather(slabs, partials, coords, counts.reshape(8, PTS), neighbours.T)
    mine = smooth(place, tot, xyz, cnt.reshape(-1), table)
    return jnp.transpose(share(mine), (0, 2, 1))


def solution(mesh):
    placed = (P("events", None, "slab", None), P(None, "slab", None), P("slab", None), P("slab"))
    return jax.shard_map(
        functools.partial(body, mesh.shape["slab"]),
        mesh=mesh, in_specs=placed, out_specs=P(None, "slab", "events"), check_vma=False,
    )
```

```python
import functools
import math

import jax
import jax.numpy as jnp
from jax import lax
from jax.experimental import pallas as pl
from jax.experimental.pallas import tpu as pltpu
from jax.sharding import PartitionSpec as P

MESH = pl.DeviceIdType.MESH
F32 = jnp.float32
BF16 = jnp.bfloat16

FACE = 256
ROWS = 4
PTS = 128
COLS = 64
WIN = 80
SLOTS = 9
SIDE = 6.0
CHUNK = 256
UNROLL = 16
AHEAD = 8
MOST = (SLOTS * PTS + CHUNK - 1) // CHUNK
NULL = (ROWS + 2) * FACE
LOG2E = math.log2(math.e)
SCALE_XY = math.sqrt(LOG2E / 128.0)
SCALE_Z = math.sqrt(LOG2E / 8.0)
ROW_ORDER = (0, 3, 1, 2)
SHIFT = SLOTS
PLACE = SHIFT + SLOTS + 1
FIRST = PLACE + SLOTS + 1
AFTER = FIRST + 1
WIDE = 32


def window(d):
    return pl.multiple_of(COLS * d - 8 + 8 * ((3 - d) // 3) - 8 * (d // 3), 8)


def swap(slab, index):
    return 2 * ((index // 2 + slab // 4) % 2) + index % 2


def place():
    slab = lax.axis_index("slab")
    return slab, swap(slab, lax.axis_index("events"))


def list_slots(slab, me, cnt, nbuf, tbuf, table):
    lane = lax.broadcasted_iota(jnp.int32, (1, FACE), 1)
    near = []
    for row in range(-1, ROWS + 1):
        which, at = (row + ROWS) // ROWS, (row + ROWS) % ROWS * 2
        line = jnp.concatenate([cnt[which, at : at + 1, :], cnt[which, at + 1 : at + 2, :]], axis=1)
        wide = jnp.broadcast_to(line, (8, FACE))
        near.append([pltpu.roll(wide, 1, 1)[:1], line, pltpu.roll(wide, FACE - 1, 1)[:1]])
    second_half = jnp.broadcast_to(me // 2, (SLOTS, PTS)) == 1
    odd = jnp.broadcast_to(me % 2, (SLOTS, PTS)) == 1
    left = lax.broadcasted_iota(jnp.int32, (SLOTS, PTS), 1) < COLS

    def own(upper, lower):
        upper = jnp.where(second_half, upper[:, PTS:], upper[:, :PTS])
        lower = jnp.where(second_half, lower[:, PTS:], lower[:, :PTS])
        upper = jnp.where(odd, pltpu.roll(upper, COLS, 1), upper)
        lower = jnp.where(odd, lower, pltpu.roll(lower, COLS, 1))
        return jnp.where(left, upper, lower)

    sources, sizes = [], []
    for row in range(ROWS):
        entry = nbuf[:, row * FACE : (row + 1) * FACE]
        step = entry - (slab * (ROWS * FACE) + row * FACE + lane)
        used = jnp.zeros((SLOTS, FACE), jnp.int32)
        for i in range(3):
            for j in range(3):
                used = jnp.where(step == (i - 1) * FACE + j - 1, near[row + i][j], used)
        sizes.append(jnp.where(entry >= 0, used, 0))
        sources.append(jnp.where(entry >= 0, entry - (slab * (ROWS * FACE) - FACE), NULL))
    which = jnp.concatenate([own(*sources[:2]), own(*sources[2:])], axis=1)
    used = jnp.concatenate([own(*sizes[:2]), own(*sizes[2:])], axis=1)
    tbuf[0:SLOTS, :] = which * 8
    starts = [jnp.zeros((1, FACE), jnp.int32)]
    for slot in range(SLOTS):
        starts.append(starts[-1] + used[slot : slot + 1, :])
    chunks = jnp.broadcast_to((starts[-1] + (CHUNK - 1)) // CHUNK, (8, FACE))
    lanes = lax.broadcasted_iota(jnp.int32, (8, FACE), 1)
    ends = chunks
    for step in (1, 2, 4, 8, 16, 32, 64, 128):
        ends = ends + jnp.where(lanes >= step, pltpu.roll(ends, step, 1), 0)
    base = (ends - chunks)[:1]
    for slot in range(SLOTS + 1):
        tbuf[SHIFT + slot : SHIFT + slot + 1, :] = starts[slot] % PTS
        tbuf[PLACE + slot : PLACE + slot + 1, :] = (base * (CHUNK // PTS) + starts[slot] // PTS) * 8
    tbuf[FIRST : FIRST + 1, :] = base
    tbuf[AFTER : AFTER + 1, :] = ends[:1]
    tbuf[AFTER + 1 : WIDE, :] = jnp.zeros((WIDE - AFTER - 1, FACE), jnp.int32)
    parts = []
    for half in range(2):
        part = tbuf[:, half * PTS : (half + 1) * PTS]
        parts += [part, pltpu.roll(part, COLS, 1)]
    table[...] = jnp.concatenate(parts, axis=0).T[:COLS]


def gather_kernel(
    slabs, parts, coords, counts, nbr, tot, xyz, cnt, table,
    nbuf, tbuf, pbuf, loc, rx1, tx2, rx2, psem, lsem, s1, r1, s2, r2, hs, hr,
):
    slab, me = place()
    high, core = me // 2, me % 2
    event = lax.axis_index("events")
    mate = 2 * (event // 2) + (1 - core)
    across = 2 * (1 - event // 2) + core

    loads = []
    for i, row in enumerate(ROW_ORDER):
        load = pltpu.make_async_copy(
            parts.at[:, :, pl.ds(row * FACE, FACE), :], pbuf.at[row], psem.at[row]
        )
        load.start()
        loads.append(load)
    mine = window(me)
    local = [
        pltpu.make_async_copy(counts, cnt.at[1], lsem.at[ROWS]),
        pltpu.make_async_copy(nbr, nbuf, lsem.at[ROWS + 1]),
    ]
    for row in range(ROWS):
        local.append(
            pltpu.make_async_copy(
                coords.at[:, pl.ds(row * FACE + mine, WIN), :], xyz.at[row + 1], lsem.at[row]
            )
        )
    for copy in local:
        copy.start()

    def beside(step):
        return {"slab": slab + step, "events": swap(slab + step, me)}

    barrier = pltpu.get_barrier_semaphore()
    for other in (mate, across):
        pl.semaphore_signal(barrier, inc=1, device_id={"events": other}, device_id_type=MESH)

    @pl.when(slab > 0)
    def _():
        pl.semaphore_signal(barrier, inc=1, device_id=beside(-1), device_id_type=MESH)

    @pl.when(slab < slabs - 1)
    def _():
        pl.semaphore_signal(barrier, inc=1, device_id=beside(1), device_id_type=MESH)

    pl.semaphore_wait(barrier, 4 - (slabs - 1 - slab) // (slabs - 1) - slab // (slabs - 1))

    def halo(up):
        row = 0 if up else ROWS - 1
        land = ROWS + 1 if up else 0
        side = 0 if up else 1
        pairs = (
            (coords.at[:, pl.ds(row * FACE + mine, WIN), :], xyz.at[land]),
            (counts, cnt.at[2 if up else 0]),
            (tot.at[row + 1], tot.at[land]),
        )
        return [
            pltpu.make_async_remote_copy(
                src_ref=src, dst_ref=dst, send_sem=hs.at[side, i], recv_sem=hr.at[side, i],
                device_id=beside(-1 if up else 1), device_id_type=MESH,
            )
            for i, (src, dst) in enumerate(pairs)
        ]

    ups, downs = halo(True), halo(False)

    @pl.when(slab > 0)
    def _():
        ups[1].start()
        ups[0].start()

    @pl.when(slab < slabs - 1)
    def _():
        downs[1].start()
        downs[0].start()

    first = {}
    for i, row in enumerate(ROW_ORDER):
        loads[i].wait()
        loc[row] = (pbuf[row, 0] + pbuf[row, 1]) + (pbuf[row, 2] + pbuf[row, 3])
        for half in range(2):
            copy = pltpu.make_async_remote_copy(
                src_ref=loc.at[row, :, pl.ds(window(2 * half + 1 - core), WIN), :],
                dst_ref=rx1.at[row, half],
                send_sem=s1.at[row, half], recv_sem=r1.at[row, half],
                device_id={"events": mate}, device_id_type=MESH,
            )
            copy.start()
            first[row, half] = copy
    second = {}
    theirs = window(2 * (1 - high) + core)
    for row in ROW_ORDER:
        for half in range(2):
            first[row, half].wait_recv()
        tx2[row] = loc[row, :, pl.ds(theirs, WIN), :] + rx1[row, 1 - high]
        copy = pltpu.make_async_remote_copy(
            src_ref=tx2.at[row], dst_ref=rx2.at[row],
            send_sem=s2.at[row], recv_sem=r2.at[row],
            device_id={"events": across}, device_id_type=MESH,
        )
        copy.start()
        second[row] = copy
    for copy in local:
        copy.wait()

    @pl.when(slab > 0)
    def _():
        downs[1].wait_recv()

    @pl.when(slab < slabs - 1)
    def _():
        ups[1].wait_recv()

    @pl.when(slab == 0)
    def _():
        cnt[0] = jnp.zeros(cnt.shape[1:], jnp.int32)

    @pl.when(slab == slabs - 1)
    def _():
        cnt[2] = jnp.zeros(cnt.shape[1:], jnp.int32)

    list_slots(slab, me, cnt, nbuf, tbuf, table)
    for row in ROW_ORDER:
        second[row].wait_recv()
        tot[row + 1] = (loc[row, :, pl.ds(mine, WIN), :] + rx1[row, high]) + rx2[row]
        if row == 0:

            @pl.when(slab > 0)
            def _():
                ups[2].start()

        if row == ROWS - 1:

            @pl.when(slab < slabs - 1)
            def _():
                downs[2].start()

    for row in ROW_ORDER:
        for half in range(2):
            first[row, half].wait_send()
        second[row].wait_send()

    @pl.when(slab > 0)
    def _():
        for copy in ups:
            copy.wait_send()
        downs[0].wait_recv()
        downs[2].wait_recv()

    @pl.when(slab < slabs - 1)
    def _():
        for copy in downs:
            copy.wait_send()
        ups[0].wait_recv()
        ups[2].wait_recv()

    @pl.when(slab == 0)
    def _():
        tot[0] = jnp.zeros(tot.shape[1:], F32)
        xyz[0] = jnp.zeros(xyz.shape[1:], F32)

    @pl.when(slab == slabs - 1)
    def _():
        tot[ROWS + 1] = jnp.zeros(tot.shape[1:], F32)
        xyz[ROWS + 1] = jnp.zeros(xyz.shape[1:], F32)


def gather(slabs, partials, coords, counts, neighbours):
    vmem = pl.BlockSpec(memory_space=pltpu.VMEM)
    hbm = pl.BlockSpec(memory_space=pltpu.HBM)
    dma = pltpu.SemaphoreType.DMA
    return pl.pallas_call(
        functools.partial(gather_kernel, slabs),
        out_shape=(
            jax.ShapeDtypeStruct((ROWS + 2, 3, WIN, PTS), F32),
            jax.ShapeDtypeStruct((ROWS + 2, 3, WIN, PTS), F32),
            jax.ShapeDtypeStruct((3, 8, PTS), jnp.int32),
            jax.ShapeDtypeStruct((COLS, ROWS * WIDE), jnp.int32),
        ),
        in_specs=[hbm, hbm, hbm, hbm],
        out_specs=(vmem, vmem, vmem, vmem),
        scratch_shapes=[
            pltpu.VMEM((SLOTS, ROWS * FACE), jnp.int32),
            pltpu.VMEM((WIDE, FACE), jnp.int32),
            pltpu.VMEM((ROWS, 4, 3, FACE, PTS), F32),
            pltpu.VMEM((ROWS, 3, FACE, PTS), F32),
            pltpu.VMEM((ROWS, 2, 3, WIN, PTS), F32),
            pltpu.VMEM((ROWS, 3, WIN, PTS), F32),
            pltpu.VMEM((ROWS, 3, WIN, PTS), F32),
            dma((ROWS,)), dma((ROWS + 2,)),
            dma((ROWS, 2)), dma((ROWS, 2)), dma((ROWS,)), dma((ROWS,)),
            dma((2, 3)), dma((2, 3)),
        ],
        compiler_params=pltpu.CompilerParams(
            collective_id=0, has_side_effects=True, vmem_limit_bytes=52 << 20
        ),
    )(partials, coords, counts, neighbours)


def split(values):
    high = values.astype(BF16)
    return high, (values - high.astype(F32)).astype(BF16)


def smooth_kernel(place, tot, xyz, cnt, table, out, src, centres, packed, acc, spread, held, staged, owner, before, now):
    slab, me = place()
    start = window(me)
    lane = lax.broadcasted_iota(jnp.int32, (8, PTS), 1)
    sub = lax.broadcasted_iota(jnp.int32, (8, PTS), 0)
    zero = jnp.zeros((8, PTS), F32)

    def build(step, _):
        row = step // (WIN // 8)
        col = pl.multiple_of(step % (WIN // 8) * 8, 8)
        tile = row * FACE + start + col
        limit = jnp.zeros((8, PTS), jnp.int32)
        for i in range(8):
            limit = jnp.where(sub == i, cnt[tile + i + (ROWS - 1) * FACE], limit)
        valid = lane < limit
        for i in range(3):
            src[pl.ds(tile * 8 + i, 8, 8), :] = jnp.where(valid, tot[row, i, pl.ds(col, 8), :], 0.0)
            src[pl.ds(tile * 8 + 4 + i, 8, 8), :] = jnp.where(valid, xyz[row, i, pl.ds(col, 8), :], 0.0)
        src[pl.ds(tile * 8 + 3, 8, 8), :] = valid.astype(F32)
        src[pl.ds(tile * 8 + 7, 8, 8), :] = zero
        return 0

    lax.fori_loop(0, (ROWS + 2) * (WIN // 8), build, 0)
    src[NULL * 8 : NULL * 8 + 8, :] = zero

    def middle(step, _):
        row, col = step // (COLS // 8), step % (COLS // 8) * 8
        for i in range(8):
            value = zero
            if i == 4:
                value = zero + ((slab * ROWS + row).astype(F32) + 0.5) * SIDE
            if i == 5:
                value = ((sub + (me * COLS + col)).astype(F32) + 0.5) * SIDE
            if i == 6:
                value = zero + 0.5 * SIDE
            centres[pl.ds(step * 64 + i, 8, 8), :] = value
        return 0

    lax.fori_loop(0, ROWS * COLS // 8, middle, 0)
    centres[ROWS * COLS * 8 : ROWS * COLS * 8 + 8, :] = zero

    tiles = ROWS * COLS
    spare = tiles * MOST

    def entry(tile):
        return (tile & (COLS - 1)) * (ROWS * WIDE) + (tile >> 6) * WIDE

    def pack(tile):
        row = entry(tile)
        for slot in range(SLOTS):
            shift = table[row + (SHIFT + slot)]
            source = src[pl.ds(pl.multiple_of(table[row + slot], 8), 8), :]
            turned = pltpu.roll(source, shift, 1)
            here = lane >= shift
            to = pl.multiple_of(table[row + (PLACE + slot)], 8)
            pltpu.store(packed.at[pl.ds(to, 8), :], turned, mask=here)
            pltpu.store(packed.at[pl.ds(to + 8, 8), :], turned, mask=jnp.logical_not(here))
        to = pl.multiple_of(table[row + (PLACE + SLOTS)], 8)
        pltpu.store(packed.at[pl.ds(to, 8), :], zero, mask=lane >= table[row + (SHIFT + SLOTS)])
        packed[pl.ds(to + 8, 8), :] = zero
        first = table[row + FIRST]
        for i in range(MOST):
            owner[first + i] = tile

    packed[spare * 16 : spare * 16 + 8, :] = zero
    packed[spare * 16 + 8 : spare * 16 + 16, :] = zero
    owner[spare] = tiles
    acc[...] = jnp.zeros_like(acc)
    scale = jnp.where(sub < 4, 1.0, jnp.where(sub < 6, SCALE_XY, SCALE_Z)).astype(F32)
    scale2 = jnp.where(sub < 4, 0.0, jnp.where(sub < 6, 2.0 * SCALE_XY, 2.0 * SCALE_Z)).astype(F32)
    minus = jnp.where((sub >= 4) & (sub < 7), -1.0, 0.0).astype(F32)
    minus = jnp.concatenate([minus, minus], axis=0).astype(BF16)

    def item(i):
        tile = now[i]
        centre = centres[pl.ds(pl.multiple_of(tile * 8, 8), 8), :]
        boths, squares = [], []
        for half in range(CHUNK // PTS):
            points = (staged[i, half * 8 : half * 8 + 8, :] - centre) * scale
            boths.append(jnp.concatenate(split(points), axis=0))
            squares.append(jnp.concatenate(split(points * points), axis=0))
        both = jnp.concatenate(boths, axis=1)
        sources = jnp.concatenate([both, both, jnp.concatenate(squares, axis=1)], axis=0)
        index = pl.multiple_of(((tile >> 6) * FACE + (tile & 63) + (FACE + me * COLS)) * 8, 8)
        query = (src[pl.ds(index, 8), :] - centre) * scale2
        q_high, q_low = split(query)
        queries = jnp.concatenate([q_high, q_high, q_low, q_low, minus], axis=0)
        return tile, both, sources, queries

    def advance(taken, made, beside):
        for i in range(UNROLL):
            at = jnp.where(taken + i < made, taken + i, spare)
            staged[i] = packed[pl.ds(pl.multiple_of(at * 16, 16), 16), :]
            now[i] = owner[at]
        todo = [item(i) for i in range(UNROLL)]
        for i in range(UNROLL):
            tile, both, sources, queries = todo[i]
            high, low = split(jnp.exp2(spread[i]))
            got = jnp.dot(held[i], jnp.concatenate([high, low], axis=1), preferred_element_type=F32)
            got = got[:, :PTS] + got[:, PTS:]
            at = pl.ds(pl.multiple_of(before[i] * 8, 8), 8)
            acc[at, :] = acc[at, :] + (got[:8] + got[8:])
            spread[i] = lax.dot_general(
                sources, queries, (((0,), (0,)), ((), ())), preferred_element_type=F32
            )
            held[i] = both
            before[i] = tile
        for i in range(UNROLL):
            beside(i)
        return jnp.minimum(taken + UNROLL, made)

    for i in range(UNROLL):
        before[i] = tiles

    def fused(step, carry):
        made, taken = carry

        def beside(i):
            if i % (UNROLL // AHEAD) == 0:
                pack(step * AHEAD + i // (UNROLL // AHEAD))

        taken = advance(taken, made, beside)
        return table[entry((step + 1) * AHEAD - 1) + AFTER], taken

    made, taken = lax.fori_loop(0, tiles // AHEAD, fused, (0, 0))
    steps = (made - taken + UNROLL - 1) // UNROLL + 1
    lax.fori_loop(0, steps, lambda _, t: advance(t, made, lambda i: None), taken)

    for pair in range(ROWS // 2):
        top = pair * 2 * COLS * 8
        flags = [
            src[pl.ds(((2 * pair + i + 1) * FACE + me * COLS) * 8 + 3, COLS, 8), :] for i in range(2)
        ]
        valid = jnp.concatenate(flags, axis=0) > 0.0
        share = 1.0 / jnp.where(valid, acc[pl.ds(top + 3, 2 * COLS, 8), :], 1.0)
        for k in range(3):
            value = jnp.where(valid, acc[pl.ds(top + k, 2 * COLS, 8), :] * share, 0.0).T
            for d in range(4):
                out[d, k, pair] = value[d * 32 : d * 32 + 32]


def smooth(place, tot, xyz, cnt, table):
    vmem = pl.BlockSpec(memory_space=pltpu.VMEM)
    smem = pl.BlockSpec(memory_space=pltpu.SMEM)
    tiles = ROWS * COLS
    most = tiles * MOST + 1
    return pl.pallas_call(
        functools.partial(smooth_kernel, place),
        out_shape=jax.ShapeDtypeStruct((4, 3, ROWS // 2, 32, PTS), F32),
        in_specs=[vmem, vmem, smem, smem],
        out_specs=vmem,
        scratch_shapes=[
            pltpu.VMEM(((NULL + 1) * 8, PTS), F32),
            pltpu.VMEM(((tiles + 1) * 8, PTS), F32),
            pltpu.VMEM((most * 16, PTS), F32),
            pltpu.VMEM(((tiles + 1) * 8, PTS), F32),
            pltpu.VMEM((UNROLL, CHUNK, PTS), F32),
            pltpu.VMEM((UNROLL, 16, CHUNK), BF16),
            pltpu.VMEM((UNROLL, 16, PTS), F32),
            pltpu.SMEM((most + 8,), jnp.int32),
            pltpu.SMEM((UNROLL,), jnp.int32),
            pltpu.SMEM((UNROLL,), jnp.int32),
        ],
        compiler_params=pltpu.CompilerParams(vmem_limit_bytes=48 << 20),
    )(tot, xyz, cnt, table)


def share_kernel(mine, out, rx, ssem, rsem):
    slab, block = place()
    me = lax.axis_index("events")
    barrier = pltpu.get_barrier_semaphore()
    for i in range(1, 4):
        pl.semaphore_signal(barrier, inc=1, device_id={"events": (me + i) % 4}, device_id_type=MESH)
    pl.semaphore_wait(barrier, 3)

    def copy(target, slot):
        return pltpu.make_async_remote_copy(
            src_ref=mine.at[target], dst_ref=rx.at[slot],
            send_sem=ssem.at[target], recv_sem=rsem.at[slot],
            device_id={"events": target}, device_id_type=MESH,
        )

    for i in (2, 3, 1):
        copy((me + i) % 4, block).start()
    rx[block] = mine[me]
    for i in (1, 3, 2):
        other = (me + i) % 4
        copy(other, swap(slab, other)).wait_recv()
    left = lax.broadcasted_iota(jnp.int32, (32, PTS), 1) < COLS
    for k in range(3):
        for pair in range(ROWS // 2):
            for half in range(2):
                a, b = rx[2 * half, k, pair], rx[2 * half + 1, k, pair]
                upper = 2 * pair * FACE + half * PTS
                lower = upper + FACE
                out[k, :, upper : upper + PTS] = jnp.where(left, a, pltpu.roll(b, COLS, 1))
                out[k, :, lower : lower + PTS] = jnp.where(left, pltpu.roll(a, COLS, 1), b)
    for i in range(1, 4):
        copy((me + i) % 4, block).wait_send()


def share(mine):
    vmem = pl.BlockSpec(memory_space=pltpu.VMEM)
    dma = pltpu.SemaphoreType.DMA
    return pl.pallas_call(
        share_kernel,
        out_shape=jax.ShapeDtypeStruct((3, 32, ROWS * FACE), F32),
        in_specs=[vmem],
        out_specs=vmem,
        scratch_shapes=[pltpu.VMEM((4, 3, ROWS // 2, 32, PTS), F32), dma((4,)), dma((4,))],
        compiler_params=pltpu.CompilerParams(
            collective_id=1, has_side_effects=True, vmem_limit_bytes=32 << 20
        ),
    )(mine)


def body(slabs, partials, coords, neighbours, counts):
    tot, xyz, cnt, table = gather(slabs, partials, coords, counts.reshape(8, PTS), neighbours.T)
    mine = smooth(place, tot, xyz, cnt.reshape(-1), table.reshape(-1))
    return jnp.transpose(share(mine), (0, 2, 1))


def solution(mesh):
    placed = (P("events", None, "slab", None), P(None, "slab", None), P("slab", None), P("slab"))
    return jax.shard_map(
        functools.partial(body, mesh.shape["slab"]),
        mesh=mesh, in_specs=placed, out_specs=P(None, "slab", "events"), check_vma=False,
    )
```

```python
import functools
import math

import jax
import jax.numpy as jnp
from jax import lax
from jax.experimental import pallas as pl
from jax.experimental.pallas import tpu as pltpu
from jax.sharding import PartitionSpec as P

MESH = pl.DeviceIdType.MESH
F32 = jnp.float32
BF16 = jnp.bfloat16

FACE = 256
ROWS = 4
PTS = 128
COLS = 64
WIN = 80
SLOTS = 9
SIDE = 6.0
CHUNK = 256
UNROLL = 16
AHEAD = 8
MOST = (SLOTS * PTS + CHUNK - 1) // CHUNK
LINES = ROWS * COLS * MOST // PTS + 1
NULL = (ROWS + 2) * FACE
LOG2E = math.log2(math.e)
SCALE_XY = math.sqrt(LOG2E / 128.0)
SCALE_Z = math.sqrt(LOG2E / 8.0)
ROW_ORDER = (0, 3, 1, 2)
SHIFT = SLOTS
PLACE = SHIFT + SLOTS + 1
AFTER = PLACE + SLOTS + 1
WIDE = 32


def window(d):
    return pl.multiple_of(COLS * d - 8 + 8 * ((3 - d) // 3) - 8 * (d // 3), 8)


def swap(slab, index):
    return 2 * ((index // 2 + slab // 4) % 2) + index % 2


def place():
    slab = lax.axis_index("slab")
    return slab, swap(slab, lax.axis_index("events"))


def list_slots(slab, me, cnt, nbuf, tbuf, table, owner):
    lane = lax.broadcasted_iota(jnp.int32, (1, FACE), 1)
    near = []
    for row in range(-1, ROWS + 1):
        which, at = (row + ROWS) // ROWS, (row + ROWS) % ROWS * 2
        line = jnp.concatenate([cnt[which, at : at + 1, :], cnt[which, at + 1 : at + 2, :]], axis=1)
        wide = jnp.broadcast_to(line, (8, FACE))
        near.append([pltpu.roll(wide, 1, 1)[:1], line, pltpu.roll(wide, FACE - 1, 1)[:1]])
    second_half = jnp.broadcast_to(me // 2, (SLOTS, PTS)) == 1
    odd = jnp.broadcast_to(me % 2, (SLOTS, PTS)) == 1
    left = lax.broadcasted_iota(jnp.int32, (SLOTS, PTS), 1) < COLS

    def own(upper, lower):
        upper = jnp.where(second_half, upper[:, PTS:], upper[:, :PTS])
        lower = jnp.where(second_half, lower[:, PTS:], lower[:, :PTS])
        upper = jnp.where(odd, pltpu.roll(upper, COLS, 1), upper)
        lower = jnp.where(odd, lower, pltpu.roll(lower, COLS, 1))
        return jnp.where(left, upper, lower)

    sources, sizes = [], []
    for row in range(ROWS):
        entry = nbuf[:, row * FACE : (row + 1) * FACE]
        step = entry - (slab * (ROWS * FACE) + row * FACE + lane)
        used = jnp.zeros((SLOTS, FACE), jnp.int32)
        for i in range(3):
            for j in range(3):
                used = jnp.where(step == (i - 1) * FACE + j - 1, near[row + i][j], used)
        sizes.append(jnp.where(entry >= 0, used, 0))
        sources.append(jnp.where(entry >= 0, entry - (slab * (ROWS * FACE) - FACE), NULL))
    which = jnp.concatenate([own(*sources[:2]), own(*sources[2:])], axis=1)
    used = jnp.concatenate([own(*sizes[:2]), own(*sizes[2:])], axis=1)
    tbuf[0:SLOTS, :] = which * 8
    starts = [jnp.zeros((1, FACE), jnp.int32)]
    for slot in range(SLOTS):
        starts.append(starts[-1] + used[slot : slot + 1, :])
    chunks = jnp.broadcast_to((starts[-1] + (CHUNK - 1)) // CHUNK, (8, FACE))
    lanes = lax.broadcasted_iota(jnp.int32, (8, FACE), 1)
    ends = chunks
    for step in (1, 2, 4, 8, 16, 32, 64, 128):
        ends = ends + jnp.where(lanes >= step, pltpu.roll(ends, step, 1), 0)
    base = (ends - chunks)[:1]
    for slot in range(SLOTS + 1):
        tbuf[SHIFT + slot : SHIFT + slot + 1, :] = starts[slot] % PTS
        tbuf[PLACE + slot : PLACE + slot + 1, :] = (base * (CHUNK // PTS) + starts[slot] // PTS) * 8
    tbuf[AFTER : AFTER + 1, :] = ends[:1]
    item = lax.broadcasted_iota(jnp.int32, (8, PTS), 1)
    turned = jnp.concatenate(
        [jnp.broadcast_to(ends[:1, half * PTS : (half + 1) * PTS], (PTS, PTS)).T for half in range(2)],
        axis=0,
    )
    for line in range(LINES):
        passed = jnp.zeros((8, PTS), jnp.int32)
        for group in range(FACE // 8):
            passed = passed + (turned[group * 8 : group * 8 + 8] <= item + line * PTS).astype(jnp.int32)
        owner[line : line + 1, :] = jnp.sum(passed, axis=0, keepdims=True)
    for half in range(2):
        for k in range(AFTER + 1):
            table[k, half : half + 1, :] = tbuf[k : k + 1, half * PTS : (half + 1) * PTS]


def gather_kernel(
    slabs, parts, coords, counts, nbr, tot, xyz, cnt, table, owner,
    nbuf, tbuf, pbuf, loc, rx1, tx2, rx2, psem, lsem, s1, r1, s2, r2, hs, hr,
):
    slab, me = place()
    high, core = me // 2, me % 2
    event = lax.axis_index("events")
    mate = 2 * (event // 2) + (1 - core)
    across = 2 * (1 - event // 2) + core

    loads = []
    for i, row in enumerate(ROW_ORDER):
        load = pltpu.make_async_copy(
            parts.at[:, :, pl.ds(row * FACE, FACE), :], pbuf.at[row], psem.at[row]
        )
        load.start()
        loads.append(load)
    mine = window(me)
    local = [
        pltpu.make_async_copy(counts, cnt.at[1], lsem.at[ROWS]),
        pltpu.make_async_copy(nbr, nbuf, lsem.at[ROWS + 1]),
    ]
    for row in range(ROWS):
        local.append(
            pltpu.make_async_copy(
                coords.at[:, pl.ds(row * FACE + mine, WIN), :], xyz.at[row + 1], lsem.at[row]
            )
        )
    for copy in local:
        copy.start()

    def beside(step):
        return {"slab": slab + step, "events": swap(slab + step, me)}

    barrier = pltpu.get_barrier_semaphore()
    for other in (mate, across):
        pl.semaphore_signal(barrier, inc=1, device_id={"events": other}, device_id_type=MESH)

    @pl.when(slab > 0)
    def _():
        pl.semaphore_signal(barrier, inc=1, device_id=beside(-1), device_id_type=MESH)

    @pl.when(slab < slabs - 1)
    def _():
        pl.semaphore_signal(barrier, inc=1, device_id=beside(1), device_id_type=MESH)

    pl.semaphore_wait(barrier, 4 - (slabs - 1 - slab) // (slabs - 1) - slab // (slabs - 1))

    def halo(up):
        row = 0 if up else ROWS - 1
        land = ROWS + 1 if up else 0
        side = 0 if up else 1
        pairs = (
            (coords.at[:, pl.ds(row * FACE + mine, WIN), :], xyz.at[land]),
            (counts, cnt.at[2 if up else 0]),
            (tot.at[row + 1], tot.at[land]),
        )
        return [
            pltpu.make_async_remote_copy(
                src_ref=src, dst_ref=dst, send_sem=hs.at[side, i], recv_sem=hr.at[side, i],
                device_id=beside(-1 if up else 1), device_id_type=MESH,
            )
            for i, (src, dst) in enumerate(pairs)
        ]

    ups, downs = halo(True), halo(False)

    @pl.when(slab > 0)
    def _():
        ups[1].start()
        ups[0].start()

    @pl.when(slab < slabs - 1)
    def _():
        downs[1].start()
        downs[0].start()

    first = {}
    for i, row in enumerate(ROW_ORDER):
        loads[i].wait()
        loc[row] = (pbuf[row, 0] + pbuf[row, 1]) + (pbuf[row, 2] + pbuf[row, 3])
        for half in range(2):
            copy = pltpu.make_async_remote_copy(
                src_ref=loc.at[row, :, pl.ds(window(2 * half + 1 - core), WIN), :],
                dst_ref=rx1.at[row, half],
                send_sem=s1.at[row, half], recv_sem=r1.at[row, half],
                device_id={"events": mate}, device_id_type=MESH,
            )
            copy.start()
            first[row, half] = copy
    second = {}
    theirs = window(2 * (1 - high) + core)
    for row in ROW_ORDER:
        for half in range(2):
            first[row, half].wait_recv()
        tx2[row] = loc[row, :, pl.ds(theirs, WIN), :] + rx1[row, 1 - high]
        copy = pltpu.make_async_remote_copy(
            src_ref=tx2.at[row], dst_ref=rx2.at[row],
            send_sem=s2.at[row], recv_sem=r2.at[row],
            device_id={"events": across}, device_id_type=MESH,
        )
        copy.start()
        second[row] = copy
    for copy in local:
        copy.wait()

    @pl.when(slab > 0)
    def _():
        downs[1].wait_recv()

    @pl.when(slab < slabs - 1)
    def _():
        ups[1].wait_recv()

    @pl.when(slab == 0)
    def _():
        cnt[0] = jnp.zeros(cnt.shape[1:], jnp.int32)

    @pl.when(slab == slabs - 1)
    def _():
        cnt[2] = jnp.zeros(cnt.shape[1:], jnp.int32)

    list_slots(slab, me, cnt, nbuf, tbuf, table, owner)
    for row in ROW_ORDER:
        second[row].wait_recv()
        tot[row + 1] = (loc[row, :, pl.ds(mine, WIN), :] + rx1[row, high]) + rx2[row]
        if row == 0:

            @pl.when(slab > 0)
            def _():
                ups[2].start()

        if row == ROWS - 1:

            @pl.when(slab < slabs - 1)
            def _():
                downs[2].start()

    for row in ROW_ORDER:
        for half in range(2):
            first[row, half].wait_send()
        second[row].wait_send()

    @pl.when(slab > 0)
    def _():
        for copy in ups:
            copy.wait_send()
        downs[0].wait_recv()
        downs[2].wait_recv()

    @pl.when(slab < slabs - 1)
    def _():
        for copy in downs:
            copy.wait_send()
        ups[0].wait_recv()
        ups[2].wait_recv()

    @pl.when(slab == 0)
    def _():
        tot[0] = jnp.zeros(tot.shape[1:], F32)
        xyz[0] = jnp.zeros(xyz.shape[1:], F32)

    @pl.when(slab == slabs - 1)
    def _():
        tot[ROWS + 1] = jnp.zeros(tot.shape[1:], F32)
        xyz[ROWS + 1] = jnp.zeros(xyz.shape[1:], F32)


def gather(slabs, partials, coords, counts, neighbours):
    vmem = pl.BlockSpec(memory_space=pltpu.VMEM)
    hbm = pl.BlockSpec(memory_space=pltpu.HBM)
    dma = pltpu.SemaphoreType.DMA
    return pl.pallas_call(
        functools.partial(gather_kernel, slabs),
        out_shape=(
            jax.ShapeDtypeStruct((ROWS + 2, 3, WIN, PTS), F32),
            jax.ShapeDtypeStruct((ROWS + 2, 3, WIN, PTS), F32),
            jax.ShapeDtypeStruct((3, 8, PTS), jnp.int32),
            jax.ShapeDtypeStruct((AFTER + 1, 8, PTS), jnp.int32),
            jax.ShapeDtypeStruct((LINES, PTS), jnp.int32),
        ),
        in_specs=[hbm, hbm, hbm, hbm],
        out_specs=(vmem, vmem, vmem, vmem, vmem),
        scratch_shapes=[
            pltpu.VMEM((SLOTS, ROWS * FACE), jnp.int32),
            pltpu.VMEM((WIDE, FACE), jnp.int32),
            pltpu.VMEM((ROWS, 4, 3, FACE, PTS), F32),
            pltpu.VMEM((ROWS, 3, FACE, PTS), F32),
            pltpu.VMEM((ROWS, 2, 3, WIN, PTS), F32),
            pltpu.VMEM((ROWS, 3, WIN, PTS), F32),
            pltpu.VMEM((ROWS, 3, WIN, PTS), F32),
            dma((ROWS,)), dma((ROWS + 2,)),
            dma((ROWS, 2)), dma((ROWS, 2)), dma((ROWS,)), dma((ROWS,)),
            dma((2, 3)), dma((2, 3)),
        ],
        compiler_params=pltpu.CompilerParams(
            collective_id=0, has_side_effects=True, vmem_limit_bytes=52 << 20
        ),
    )(partials, coords, counts, neighbours)


def split(values):
    high = values.astype(BF16)
    return high, (values - high.astype(F32)).astype(BF16)


def smooth_kernel(place, tot, xyz, cnt, owner, rows, out, src, centres, packed, acc, spread, held, staged, before, now, sem, *table):
    slab, me = place()
    loads = [
        pltpu.make_async_copy(rows.at[k, 0:2, :], table[k], sem.at[k]) for k in range(AFTER + 1)
    ]
    for load in loads:
        load.start()
    start = window(me)
    lane = lax.broadcasted_iota(jnp.int32, (8, PTS), 1)
    sub = lax.broadcasted_iota(jnp.int32, (8, PTS), 0)
    zero = jnp.zeros((8, PTS), F32)

    def build(step, _):
        row = step // (WIN // 8)
        col = pl.multiple_of(step % (WIN // 8) * 8, 8)
        tile = row * FACE + start + col
        limit = jnp.zeros((8, PTS), jnp.int32)
        for i in range(8):
            limit = jnp.where(sub == i, cnt[tile + i + (ROWS - 1) * FACE], limit)
        valid = lane < limit
        for i in range(3):
            src[pl.ds(tile * 8 + i, 8, 8), :] = jnp.where(valid, tot[row, i, pl.ds(col, 8), :], 0.0)
            src[pl.ds(tile * 8 + 4 + i, 8, 8), :] = jnp.where(valid, xyz[row, i, pl.ds(col, 8), :], 0.0)
        src[pl.ds(tile * 8 + 3, 8, 8), :] = valid.astype(F32)
        src[pl.ds(tile * 8 + 7, 8, 8), :] = zero
        return 0

    lax.fori_loop(0, (ROWS + 2) * (WIN // 8), build, 0, unroll=4)
    src[NULL * 8 : NULL * 8 + 8, :] = zero

    def middle(step, _):
        row, col = step // (COLS // 8), step % (COLS // 8) * 8
        for i in range(8):
            value = zero
            if i == 4:
                value = zero + ((slab * ROWS + row).astype(F32) + 0.5) * SIDE
            if i == 5:
                value = ((sub + (me * COLS + col)).astype(F32) + 0.5) * SIDE
            if i == 6:
                value = zero + 0.5 * SIDE
            centres[pl.ds(step * 64 + i, 8, 8), :] = value
        return 0

    lax.fori_loop(0, ROWS * COLS // 8, middle, 0, unroll=4)
    centres[ROWS * COLS * 8 : ROWS * COLS * 8 + 8, :] = zero

    tiles = ROWS * COLS
    spare = tiles * MOST

    def look(k, tile):
        return table[k][tile >> 7, tile & (PTS - 1)]

    def pack(tile):
        for slot in range(SLOTS):
            shift = look(SHIFT + slot, tile)
            source = src[pl.ds(pl.multiple_of(look(slot, tile), 8), 8), :]
            turned = pltpu.roll(source, shift, 1)
            here = lane >= shift
            to = pl.multiple_of(look(PLACE + slot, tile), 8)
            pltpu.store(packed.at[pl.ds(to, 8), :], turned, mask=here)
            pltpu.store(packed.at[pl.ds(to + 8, 8), :], turned, mask=jnp.logical_not(here))
        to = pl.multiple_of(look(PLACE + SLOTS, tile), 8)
        pltpu.store(packed.at[pl.ds(to, 8), :], zero, mask=lane >= look(SHIFT + SLOTS, tile))
        packed[pl.ds(to + 8, 8), :] = zero

    packed[spare * 16 : spare * 16 + 8, :] = zero
    packed[spare * 16 + 8 : spare * 16 + 16, :] = zero
    for load in loads:
        load.wait()
    acc[...] = jnp.zeros_like(acc)
    scale = jnp.where(sub < 4, 1.0, jnp.where(sub < 6, SCALE_XY, SCALE_Z)).astype(F32)
    scale2 = jnp.where(sub < 4, 0.0, jnp.where(sub < 6, 2.0 * SCALE_XY, 2.0 * SCALE_Z)).astype(F32)
    minus = jnp.where((sub >= 4) & (sub < 7), -1.0, 0.0).astype(F32)
    minus = jnp.concatenate([minus, minus], axis=0).astype(BF16)

    def item(i):
        tile = now[i]
        centre = centres[pl.ds(pl.multiple_of(tile * 8, 8), 8), :]
        boths, squares = [], []
        for half in range(CHUNK // PTS):
            points = (staged[i, half * 8 : half * 8 + 8, :] - centre) * scale
            boths.append(jnp.concatenate(split(points), axis=0))
            squares.append(jnp.concatenate(split(points * points), axis=0))
        both = jnp.concatenate(boths, axis=1)
        sources = jnp.concatenate([both, both, jnp.concatenate(squares, axis=1)], axis=0)
        index = pl.multiple_of(((tile >> 6) * FACE + (tile & 63) + (FACE + me * COLS)) * 8, 8)
        query = (src[pl.ds(index, 8), :] - centre) * scale2
        q_high, q_low = split(query)
        queries = jnp.concatenate([q_high, q_high, q_low, q_low, minus], axis=0)
        return tile, both, sources, queries

    def advance(taken, made, beside):
        for i in range(UNROLL):
            at = jnp.where(taken + i < made, taken + i, spare)
            staged[i] = packed[pl.ds(pl.multiple_of(at * 16, 16), 16), :]
            now[i] = owner[at >> 7, at & (PTS - 1)]
        todo = [item(i) for i in range(UNROLL)]
        for i in range(UNROLL):
            tile, both, sources, queries = todo[i]
            high, low = split(jnp.exp2(spread[i]))
            got = jnp.dot(held[i], jnp.concatenate([high, low], axis=1), preferred_element_type=F32)
            got = got[:, :PTS] + got[:, PTS:]
            at = pl.ds(pl.multiple_of(before[i] * 8, 8), 8)
            acc[at, :] = acc[at, :] + (got[:8] + got[8:])
            spread[i] = lax.dot_general(
                sources, queries, (((0,), (0,)), ((), ())), preferred_element_type=F32
            )
            held[i] = both
            before[i] = tile
        for i in range(UNROLL):
            beside(i)
        return jnp.minimum(taken + UNROLL, made)

    for i in range(UNROLL):
        before[i] = tiles

    def fused(step, carry):
        made, taken = carry

        def beside(i):
            if i % (UNROLL // AHEAD) == 0:
                pack(step * AHEAD + i // (UNROLL // AHEAD))

        taken = advance(taken, made, beside)
        return look(AFTER, (step + 1) * AHEAD - 1), taken

    made, taken = lax.fori_loop(0, tiles // AHEAD, fused, (0, 0))
    steps = (made - taken + UNROLL - 1) // UNROLL + 1
    lax.fori_loop(0, steps, lambda _, t: advance(t, made, lambda i: None), taken)

    for pair in range(ROWS // 2):
        top = pair * 2 * COLS * 8
        flags = [
            src[pl.ds(((2 * pair + i + 1) * FACE + me * COLS) * 8 + 3, COLS, 8), :] for i in range(2)
        ]
        valid = jnp.concatenate(flags, axis=0) > 0.0
        share = 1.0 / jnp.where(valid, acc[pl.ds(top + 3, 2 * COLS, 8), :], 1.0)
        for k in range(3):
            value = jnp.where(valid, acc[pl.ds(top + k, 2 * COLS, 8), :] * share, 0.0).T
            for d in range(4):
                out[d, k, pair] = value[d * 32 : d * 32 + 32]


def smooth(place, tot, xyz, cnt, owner, table):
    vmem = pl.BlockSpec(memory_space=pltpu.VMEM)
    smem = pl.BlockSpec(memory_space=pltpu.SMEM)
    tiles = ROWS * COLS
    most = tiles * MOST + 1
    return pl.pallas_call(
        functools.partial(smooth_kernel, place),
        out_shape=jax.ShapeDtypeStruct((4, 3, ROWS // 2, 32, PTS), F32),
        in_specs=[vmem, vmem, smem, smem, vmem],
        out_specs=vmem,
        scratch_shapes=[
            pltpu.VMEM(((NULL + 1) * 8, PTS), F32),
            pltpu.VMEM(((tiles + 1) * 8, PTS), F32),
            pltpu.VMEM((most * 16, PTS), F32),
            pltpu.VMEM(((tiles + 1) * 8, PTS), F32),
            pltpu.VMEM((UNROLL, CHUNK, PTS), F32),
            pltpu.VMEM((UNROLL, 16, CHUNK), BF16),
            pltpu.VMEM((UNROLL, 16, PTS), F32),
            pltpu.SMEM((UNROLL,), jnp.int32),
            pltpu.SMEM((UNROLL,), jnp.int32),
            pltpu.SemaphoreType.DMA((AFTER + 1,)),
            *[pltpu.SMEM((2, PTS), jnp.int32)] * (AFTER + 1),
        ],
        compiler_params=pltpu.CompilerParams(vmem_limit_bytes=48 << 20),
    )(tot, xyz, cnt, owner, table)


def share_kernel(mine, out, rx, ssem, rsem):
    slab, block = place()
    me = lax.axis_index("events")
    barrier = pltpu.get_barrier_semaphore()
    for i in range(1, 4):
        pl.semaphore_signal(barrier, inc=1, device_id={"events": (me + i) % 4}, device_id_type=MESH)
    pl.semaphore_wait(barrier, 3)

    def copy(target, slot):
        return pltpu.make_async_remote_copy(
            src_ref=mine.at[target], dst_ref=rx.at[slot],
            send_sem=ssem.at[target], recv_sem=rsem.at[slot],
            device_id={"events": target}, device_id_type=MESH,
        )

    for i in (2, 3, 1):
        copy((me + i) % 4, block).start()
    rx[block] = mine[me]
    for i in (1, 3, 2):
        other = (me + i) % 4
        copy(other, swap(slab, other)).wait_recv()
    left = lax.broadcasted_iota(jnp.int32, (32, PTS), 1) < COLS
    for k in range(3):
        for pair in range(ROWS // 2):
            for half in range(2):
                a, b = rx[2 * half, k, pair], rx[2 * half + 1, k, pair]
                upper = 2 * pair * FACE + half * PTS
                lower = upper + FACE
                out[k, :, upper : upper + PTS] = jnp.where(left, a, pltpu.roll(b, COLS, 1))
                out[k, :, lower : lower + PTS] = jnp.where(left, pltpu.roll(a, COLS, 1), b)
    for i in range(1, 4):
        copy((me + i) % 4, block).wait_send()


def share(mine):
    vmem = pl.BlockSpec(memory_space=pltpu.VMEM)
    dma = pltpu.SemaphoreType.DMA
    return pl.pallas_call(
        share_kernel,
        out_shape=jax.ShapeDtypeStruct((3, 32, ROWS * FACE), F32),
        in_specs=[vmem],
        out_specs=vmem,
        scratch_shapes=[pltpu.VMEM((4, 3, ROWS // 2, 32, PTS), F32), dma((4,)), dma((4,))],
        compiler_params=pltpu.CompilerParams(
            collective_id=1, has_side_effects=True, vmem_limit_bytes=32 << 20
        ),
    )(mine)


def body(slabs, partials, coords, neighbours, counts):
    tot, xyz, cnt, table, owner = gather(slabs, partials, coords, counts.reshape(8, PTS), neighbours.T)
    mine = smooth(place, tot, xyz, cnt.reshape(-1), owner, table)
    return jnp.transpose(share(mine), (0, 2, 1))


def solution(mesh):
    placed = (P("events", None, "slab", None), P(None, "slab", None), P("slab", None), P("slab"))
    return jax.shard_map(
        functools.partial(body, mesh.shape["slab"]),
        mesh=mesh, in_specs=placed, out_specs=P(None, "slab", "events"), check_vma=False,
    )
```

```python
import functools
import math

import jax
import jax.numpy as jnp
from jax import lax
from jax.experimental import pallas as pl
from jax.experimental.pallas import tpu as pltpu
from jax.sharding import PartitionSpec as P

MESH = pl.DeviceIdType.MESH
F32 = jnp.float32
BF16 = jnp.bfloat16

FACE = 256
ROWS = 4
PTS = 128
COLS = 64
WIN = 80
SLOTS = 9
SIDE = 6.0
CHUNK = 256
UNROLL = 16
AHEAD = 8
MOST = (SLOTS * PTS + CHUNK - 1) // CHUNK
LINES = ROWS * COLS * MOST // PTS + 1
NULL = (ROWS + 2) * FACE
LOG2E = math.log2(math.e)
SCALE_XY = math.sqrt(LOG2E / 128.0)
SCALE_Z = math.sqrt(LOG2E / 8.0)
ROW_ORDER = (0, 3, 1, 2)
SHIFT = SLOTS
PLACE = SHIFT + SLOTS + 1
AFTER = PLACE + SLOTS + 1
WIDE = 32


def window(d):
    return pl.multiple_of(COLS * d - 8 + 8 * ((3 - d) // 3) - 8 * (d // 3), 8)


def swap(slab, index):
    return 2 * ((index // 2 + slab // 4) % 2) + index % 2


def place():
    slab = lax.axis_index("slab")
    return slab, swap(slab, lax.axis_index("events"))


def list_slots(slab, me, sizes, nbuf, tbuf, table, owner):
    lane = lax.broadcasted_iota(jnp.int32, (1, FACE), 1)
    near = []
    for row in range(-1, ROWS + 1):
        at = (row + ROWS) % ROWS * FACE
        line = sizes[(row + ROWS) // ROWS, 0:1, at : at + FACE]
        wide = jnp.broadcast_to(line, (8, FACE))
        near.append([pltpu.roll(wide, 1, 1)[:1], line, pltpu.roll(wide, FACE - 1, 1)[:1]])
    second_half = jnp.broadcast_to(me // 2, (SLOTS, PTS)) == 1
    odd = jnp.broadcast_to(me % 2, (SLOTS, PTS)) == 1
    left = lax.broadcasted_iota(jnp.int32, (SLOTS, PTS), 1) < COLS

    def own(upper, lower):
        upper = jnp.where(second_half, upper[:, PTS:], upper[:, :PTS])
        lower = jnp.where(second_half, lower[:, PTS:], lower[:, :PTS])
        upper = jnp.where(odd, pltpu.roll(upper, COLS, 1), upper)
        lower = jnp.where(odd, lower, pltpu.roll(lower, COLS, 1))
        return jnp.where(left, upper, lower)

    sources, lengths = [], []
    for row in range(ROWS):
        entry = nbuf[:SLOTS, row * FACE : (row + 1) * FACE]
        step = entry - (slab * (ROWS * FACE) + row * FACE + lane)
        used = jnp.zeros((SLOTS, FACE), jnp.int32)
        for i in range(3):
            for j in range(3):
                used = jnp.where(step == (i - 1) * FACE + j - 1, near[row + i][j], used)
        lengths.append(jnp.where(entry >= 0, used, 0))
        sources.append(jnp.where(entry >= 0, entry - (slab * (ROWS * FACE) - FACE), NULL))
    which = jnp.concatenate([own(*sources[:2]), own(*sources[2:])], axis=1)
    used = jnp.concatenate([own(*lengths[:2]), own(*lengths[2:])], axis=1)
    tbuf[0:SLOTS, :] = which * 8
    starts = [jnp.zeros((1, FACE), jnp.int32)]
    for slot in range(SLOTS):
        starts.append(starts[-1] + used[slot : slot + 1, :])
    chunks = jnp.broadcast_to((starts[-1] + (CHUNK - 1)) // CHUNK, (8, FACE))
    lanes = lax.broadcasted_iota(jnp.int32, (8, FACE), 1)
    ends = chunks
    for step in (1, 2, 4, 8, 16, 32, 64, 128):
        ends = ends + jnp.where(lanes >= step, pltpu.roll(ends, step, 1), 0)
    base = (ends - chunks)[:1]
    for slot in range(SLOTS + 1):
        tbuf[SHIFT + slot : SHIFT + slot + 1, :] = starts[slot] % PTS
        tbuf[PLACE + slot : PLACE + slot + 1, :] = (base * (CHUNK // PTS) + starts[slot] // PTS) * 8
    tbuf[AFTER : AFTER + 1, :] = ends[:1]
    item = lax.broadcasted_iota(jnp.int32, (8, PTS), 1)
    turned = jnp.concatenate(
        [jnp.broadcast_to(ends[:1, half * PTS : (half + 1) * PTS], (PTS, PTS)).T for half in range(2)],
        axis=0,
    )
    for line in range(LINES):
        passed = jnp.zeros((8, PTS), jnp.int32)
        for group in range(FACE // 8):
            passed = passed + (turned[group * 8 : group * 8 + 8] <= item + line * PTS).astype(jnp.int32)
        owner[line : line + 1, :] = jnp.sum(passed, axis=0, keepdims=True)
    for half in range(2):
        for k in range(AFTER + 1):
            table[k, half : half + 1, :] = tbuf[k : k + 1, half * PTS : (half + 1) * PTS]


def gather_kernel(
    slabs, parts, coords, lists, tot, xyz, cnt, table, owner,
    sizes, nbuf, tbuf, pbuf, loc, rx1, tx2, rx2, psem, lsem, s1, r1, s2, r2, hs, hr,
):
    slab, me = place()
    high, core = me // 2, me % 2
    event = lax.axis_index("events")
    mate = 2 * (event // 2) + (1 - core)
    across = 2 * (1 - event // 2) + core

    loads = []
    for i, row in enumerate(ROW_ORDER):
        load = pltpu.make_async_copy(
            parts.at[:, :, pl.ds(row * FACE, FACE), :], pbuf.at[row], psem.at[row]
        )
        load.start()
        loads.append(load)
    mine = window(me)
    local = [
        pltpu.make_async_copy(lists.at[16:24, :], sizes.at[1], lsem.at[ROWS]),
        pltpu.make_async_copy(lists.at[0:16, :], nbuf, lsem.at[ROWS + 1]),
    ]
    for row in range(ROWS):
        local.append(
            pltpu.make_async_copy(
                coords.at[:, pl.ds(row * FACE + mine, WIN), :], xyz.at[row + 1], lsem.at[row]
            )
        )
    for copy in local:
        copy.start()

    def beside(step):
        return {"slab": slab + step, "events": swap(slab + step, me)}

    barrier = pltpu.get_barrier_semaphore()
    for other in (mate, across):
        pl.semaphore_signal(barrier, inc=1, device_id={"events": other}, device_id_type=MESH)

    @pl.when(slab > 0)
    def _():
        pl.semaphore_signal(barrier, inc=1, device_id=beside(-1), device_id_type=MESH)

    @pl.when(slab < slabs - 1)
    def _():
        pl.semaphore_signal(barrier, inc=1, device_id=beside(1), device_id_type=MESH)

    pl.semaphore_wait(barrier, 4 - (slabs - 1 - slab) // (slabs - 1) - slab // (slabs - 1))

    def halo(up):
        row = 0 if up else ROWS - 1
        land = ROWS + 1 if up else 0
        side = 0 if up else 1
        pairs = (
            (coords.at[:, pl.ds(row * FACE + mine, WIN), :], xyz.at[land]),
            (lists.at[16:24, :], sizes.at[2 if up else 0]),
            (tot.at[row + 1], tot.at[land]),
        )
        return [
            pltpu.make_async_remote_copy(
                src_ref=src, dst_ref=dst, send_sem=hs.at[side, i], recv_sem=hr.at[side, i],
                device_id=beside(-1 if up else 1), device_id_type=MESH,
            )
            for i, (src, dst) in enumerate(pairs)
        ]

    ups, downs = halo(True), halo(False)

    @pl.when(slab > 0)
    def _():
        ups[1].start()
        ups[0].start()

    @pl.when(slab < slabs - 1)
    def _():
        downs[1].start()
        downs[0].start()

    first, second = {}, {}
    theirs = window(2 * (1 - high) + core)

    def cross(row):
        for half in range(2):
            first[row, half].wait_recv()
        tx2[row] = loc[row, :, pl.ds(theirs, WIN), :] + rx1[row, 1 - high]
        second[row] = pltpu.make_async_remote_copy(
            src_ref=tx2.at[row], dst_ref=rx2.at[row],
            send_sem=s2.at[row], recv_sem=r2.at[row],
            device_id={"events": across}, device_id_type=MESH,
        )
        second[row].start()

    for i, row in enumerate(ROW_ORDER):
        loads[i].wait()
        loc[row] = (pbuf[row, 0] + pbuf[row, 1]) + (pbuf[row, 2] + pbuf[row, 3])
        for half in range(2):
            first[row, half] = pltpu.make_async_remote_copy(
                src_ref=loc.at[row, :, pl.ds(window(2 * half + 1 - core), WIN), :],
                dst_ref=rx1.at[row, half],
                send_sem=s1.at[row, half], recv_sem=r1.at[row, half],
                device_id={"events": mate}, device_id_type=MESH,
            )
            first[row, half].start()
        if i > 0:
            cross(ROW_ORDER[i - 1])
    cross(ROW_ORDER[-1])
    for copy in local:
        copy.wait()

    @pl.when(slab > 0)
    def _():
        downs[1].wait_recv()

    @pl.when(slab < slabs - 1)
    def _():
        ups[1].wait_recv()

    @pl.when(slab == 0)
    def _():
        sizes[0] = jnp.zeros(sizes.shape[1:], jnp.int32)

    @pl.when(slab == slabs - 1)
    def _():
        sizes[2] = jnp.zeros(sizes.shape[1:], jnp.int32)

    for i in range(3):
        for j in range(8):
            cnt[i, j : j + 1, :] = sizes[i, 0:1, j * PTS : (j + 1) * PTS]
    list_slots(slab, me, sizes, nbuf, tbuf, table, owner)
    for row in ROW_ORDER:
        second[row].wait_recv()
        tot[row + 1] = (loc[row, :, pl.ds(mine, WIN), :] + rx1[row, high]) + rx2[row]
        if row == 0:

            @pl.when(slab > 0)
            def _():
                ups[2].start()

        if row == ROWS - 1:

            @pl.when(slab < slabs - 1)
            def _():
                downs[2].start()

    for row in ROW_ORDER:
        for half in range(2):
            first[row, half].wait_send()
        second[row].wait_send()

    @pl.when(slab > 0)
    def _():
        for copy in ups:
            copy.wait_send()
        downs[0].wait_recv()
        downs[2].wait_recv()

    @pl.when(slab < slabs - 1)
    def _():
        for copy in downs:
            copy.wait_send()
        ups[0].wait_recv()
        ups[2].wait_recv()

    @pl.when(slab == 0)
    def _():
        tot[0] = jnp.zeros(tot.shape[1:], F32)
        xyz[0] = jnp.zeros(xyz.shape[1:], F32)

    @pl.when(slab == slabs - 1)
    def _():
        tot[ROWS + 1] = jnp.zeros(tot.shape[1:], F32)
        xyz[ROWS + 1] = jnp.zeros(xyz.shape[1:], F32)


def gather(slabs, partials, coords, lists):
    vmem = pl.BlockSpec(memory_space=pltpu.VMEM)
    hbm = pl.BlockSpec(memory_space=pltpu.HBM)
    dma = pltpu.SemaphoreType.DMA
    return pl.pallas_call(
        functools.partial(gather_kernel, slabs),
        out_shape=(
            jax.ShapeDtypeStruct((ROWS + 2, 3, WIN, PTS), F32),
            jax.ShapeDtypeStruct((ROWS + 2, 3, WIN, PTS), F32),
            jax.ShapeDtypeStruct((3, 8, PTS), jnp.int32),
            jax.ShapeDtypeStruct((AFTER + 1, 8, PTS), jnp.int32),
            jax.ShapeDtypeStruct((LINES, PTS), jnp.int32),
        ),
        in_specs=[hbm, hbm, hbm],
        out_specs=(vmem, vmem, vmem, vmem, vmem),
        scratch_shapes=[
            pltpu.VMEM((3, 8, ROWS * FACE), jnp.int32),
            pltpu.VMEM((16, ROWS * FACE), jnp.int32),
            pltpu.VMEM((WIDE, FACE), jnp.int32),
            pltpu.VMEM((ROWS, 4, 3, FACE, PTS), F32),
            pltpu.VMEM((ROWS, 3, FACE, PTS), F32),
            pltpu.VMEM((ROWS, 2, 3, WIN, PTS), F32),
            pltpu.VMEM((ROWS, 3, WIN, PTS), F32),
            pltpu.VMEM((ROWS, 3, WIN, PTS), F32),
            dma((ROWS,)), dma((ROWS + 2,)),
            dma((ROWS, 2)), dma((ROWS, 2)), dma((ROWS,)), dma((ROWS,)),
            dma((2, 3)), dma((2, 3)),
        ],
        compiler_params=pltpu.CompilerParams(
            collective_id=0, has_side_effects=True, vmem_limit_bytes=52 << 20
        ),
    )(partials, coords, lists)


def split(values):
    high = values.astype(BF16)
    return high, (values - high.astype(F32)).astype(BF16)


def smooth_kernel(place, tot, xyz, cnt, owner, rows, out, src, centres, packed, acc, spread, held, staged, before, now, sem, *table):
    slab, me = place()
    loads = [
        pltpu.make_async_copy(rows.at[k, 0:2, :], table[k], sem.at[k]) for k in range(AFTER + 1)
    ]
    for load in loads:
        load.start()
    start = window(me)
    lane = lax.broadcasted_iota(jnp.int32, (8, PTS), 1)
    sub = lax.broadcasted_iota(jnp.int32, (8, PTS), 0)
    zero = jnp.zeros((8, PTS), F32)

    def build(step, _):
        row = step // (WIN // 8)
        col = pl.multiple_of(step % (WIN // 8) * 8, 8)
        tile = row * FACE + start + col
        limit = jnp.zeros((8, PTS), jnp.int32)
        for i in range(8):
            limit = jnp.where(sub == i, cnt[tile + i + (ROWS - 1) * FACE], limit)
        valid = lane < limit
        for i in range(3):
            src[pl.ds(tile * 8 + i, 8, 8), :] = jnp.where(valid, tot[row, i, pl.ds(col, 8), :], 0.0)
            src[pl.ds(tile * 8 + 4 + i, 8, 8), :] = jnp.where(valid, xyz[row, i, pl.ds(col, 8), :], 0.0)
        src[pl.ds(tile * 8 + 3, 8, 8), :] = valid.astype(F32)
        src[pl.ds(tile * 8 + 7, 8, 8), :] = zero
        return 0

    lax.fori_loop(0, (ROWS + 2) * (WIN // 8), build, 0, unroll=4)
    src[NULL * 8 : NULL * 8 + 8, :] = zero

    def middle(step, _):
        row, col = step // (COLS // 8), step % (COLS // 8) * 8
        for i in range(8):
            value = zero
            if i == 4:
                value = zero + ((slab * ROWS + row).astype(F32) + 0.5) * SIDE
            if i == 5:
                value = ((sub + (me * COLS + col)).astype(F32) + 0.5) * SIDE
            if i == 6:
                value = zero + 0.5 * SIDE
            centres[pl.ds(step * 64 + i, 8, 8), :] = value
        return 0

    lax.fori_loop(0, ROWS * COLS // 8, middle, 0, unroll=4)
    centres[ROWS * COLS * 8 : ROWS * COLS * 8 + 8, :] = zero

    tiles = ROWS * COLS
    spare = tiles * MOST

    def look(k, tile):
        return table[k][tile >> 7, tile & (PTS - 1)]

    def pack(tile):
        for slot in range(SLOTS):
            shift = look(SHIFT + slot, tile)
            source = src[pl.ds(pl.multiple_of(look(slot, tile), 8), 8), :]
            turned = pltpu.roll(source, shift, 1)
            here = lane >= shift
            to = pl.multiple_of(look(PLACE + slot, tile), 8)
            pltpu.store(packed.at[pl.ds(to, 8), :], turned, mask=here)
            pltpu.store(packed.at[pl.ds(to + 8, 8), :], turned, mask=jnp.logical_not(here))
        to = pl.multiple_of(look(PLACE + SLOTS, tile), 8)
        pltpu.store(packed.at[pl.ds(to, 8), :], zero, mask=lane >= look(SHIFT + SLOTS, tile))
        packed[pl.ds(to + 8, 8), :] = zero

    packed[spare * 16 : spare * 16 + 8, :] = zero
    packed[spare * 16 + 8 : spare * 16 + 16, :] = zero
    for load in loads:
        load.wait()
    acc[...] = jnp.zeros_like(acc)
    scale = jnp.where(sub < 4, 1.0, jnp.where(sub < 6, SCALE_XY, SCALE_Z)).astype(F32)
    scale2 = jnp.where(sub < 4, 0.0, jnp.where(sub < 6, 2.0 * SCALE_XY, 2.0 * SCALE_Z)).astype(F32)
    minus = jnp.where((sub >= 4) & (sub < 7), -1.0, 0.0).astype(F32)
    minus = jnp.concatenate([minus, minus], axis=0).astype(BF16)

    def item(i):
        tile = now[i]
        centre = centres[pl.ds(pl.multiple_of(tile * 8, 8), 8), :]
        boths, squares = [], []
        for half in range(CHUNK // PTS):
            points = (staged[i, half * 8 : half * 8 + 8, :] - centre) * scale
            boths.append(jnp.concatenate(split(points), axis=0))
            squares.append(jnp.concatenate(split(points * points), axis=0))
        both = jnp.concatenate(boths, axis=1)
        sources = jnp.concatenate([both, both, jnp.concatenate(squares, axis=1)], axis=0)
        index = pl.multiple_of(((tile >> 6) * FACE + (tile & 63) + (FACE + me * COLS)) * 8, 8)
        query = (src[pl.ds(index, 8), :] - centre) * scale2
        q_high, q_low = split(query)
        queries = jnp.concatenate([q_high, q_high, q_low, q_low, minus], axis=0)
        return tile, both, sources, queries

    def advance(taken, made, beside):
        for i in range(UNROLL):
            at = jnp.where(taken + i < made, taken + i, spare)
            staged[i] = packed[pl.ds(pl.multiple_of(at * 16, 16), 16), :]
            now[i] = owner[at >> 7, at & (PTS - 1)]
        todo = [item(i) for i in range(UNROLL)]
        for i in range(UNROLL):
            tile, both, sources, queries = todo[i]
            high, low = split(jnp.exp2(spread[i]))
            got = jnp.dot(held[i], jnp.concatenate([high, low], axis=1), preferred_element_type=F32)
            got = got[:, :PTS] + got[:, PTS:]
            at = pl.ds(pl.multiple_of(before[i] * 8, 8), 8)
            acc[at, :] = acc[at, :] + (got[:8] + got[8:])
            spread[i] = lax.dot_general(
                sources, queries, (((0,), (0,)), ((), ())), preferred_element_type=F32
            )
            held[i] = both
            before[i] = tile
            beside(i)
        return jnp.minimum(taken + UNROLL, made)

    for i in range(UNROLL):
        before[i] = tiles

    def fused(step, carry):
        made, taken = carry

        def beside(i):
            if i % (UNROLL // AHEAD) == 0:
                pack(step * AHEAD + i // (UNROLL // AHEAD))

        taken = advance(taken, made, beside)
        return look(AFTER, (step + 1) * AHEAD - 1), taken

    made, taken = lax.fori_loop(0, tiles // AHEAD, fused, (0, 0))
    steps = (made - taken + UNROLL - 1) // UNROLL + 1
    lax.fori_loop(0, steps, lambda _, t: advance(t, made, lambda i: None), taken)

    for pair in range(ROWS // 2):
        top = pair * 2 * COLS * 8
        flags = [
            src[pl.ds(((2 * pair + i + 1) * FACE + me * COLS) * 8 + 3, COLS, 8), :] for i in range(2)
        ]
        valid = jnp.concatenate(flags, axis=0) > 0.0
        share = 1.0 / jnp.where(valid, acc[pl.ds(top + 3, 2 * COLS, 8), :], 1.0)
        for k in range(3):
            value = jnp.where(valid, acc[pl.ds(top + k, 2 * COLS, 8), :] * share, 0.0).T
            for d in range(4):
                out[d, k, pair] = value[d * 32 : d * 32 + 32]


def smooth(place, tot, xyz, cnt, owner, table):
    vmem = pl.BlockSpec(memory_space=pltpu.VMEM)
    smem = pl.BlockSpec(memory_space=pltpu.SMEM)
    tiles = ROWS * COLS
    most = tiles * MOST + 1
    return pl.pallas_call(
        functools.partial(smooth_kernel, place),
        out_shape=jax.ShapeDtypeStruct((4, 3, ROWS // 2, 32, PTS), F32),
        in_specs=[vmem, vmem, smem, smem, vmem],
        out_specs=vmem,
        scratch_shapes=[
            pltpu.VMEM(((NULL + 1) * 8, PTS), F32),
            pltpu.VMEM(((tiles + 1) * 8, PTS), F32),
            pltpu.VMEM((most * 16, PTS), F32),
            pltpu.VMEM(((tiles + 1) * 8, PTS), F32),
            pltpu.VMEM((UNROLL, CHUNK, PTS), F32),
            pltpu.VMEM((UNROLL, 16, CHUNK), BF16),
            pltpu.VMEM((UNROLL, 16, PTS), F32),
            pltpu.SMEM((UNROLL,), jnp.int32),
            pltpu.SMEM((UNROLL,), jnp.int32),
            pltpu.SemaphoreType.DMA((AFTER + 1,)),
            *[pltpu.SMEM((2, PTS), jnp.int32)] * (AFTER + 1),
        ],
        compiler_params=pltpu.CompilerParams(vmem_limit_bytes=48 << 20),
    )(tot, xyz, cnt, owner, table)


def share_kernel(mine, out, rx, ssem, rsem):
    slab, block = place()
    me = lax.axis_index("events")
    barrier = pltpu.get_barrier_semaphore()
    for i in range(1, 4):
        pl.semaphore_signal(barrier, inc=1, device_id={"events": (me + i) % 4}, device_id_type=MESH)
    pl.semaphore_wait(barrier, 3)

    def copy(target, slot):
        return pltpu.make_async_remote_copy(
            src_ref=mine.at[target], dst_ref=rx.at[slot],
            send_sem=ssem.at[target], recv_sem=rsem.at[slot],
            device_id={"events": target}, device_id_type=MESH,
        )

    for i in (2, 3, 1):
        copy((me + i) % 4, block).start()
    rx[block] = mine[me]
    for i in (1, 3, 2):
        other = (me + i) % 4
        copy(other, swap(slab, other)).wait_recv()
    left = lax.broadcasted_iota(jnp.int32, (32, PTS), 1) < COLS
    for k in range(3):
        for pair in range(ROWS // 2):
            for half in range(2):
                a, b = rx[2 * half, k, pair], rx[2 * half + 1, k, pair]
                upper = 2 * pair * FACE + half * PTS
                lower = upper + FACE
                out[k, :, upper : upper + PTS] = jnp.where(left, a, pltpu.roll(b, COLS, 1))
                out[k, :, lower : lower + PTS] = jnp.where(left, pltpu.roll(a, COLS, 1), b)
    for i in range(1, 4):
        copy((me + i) % 4, block).wait_send()


def share(mine):
    vmem = pl.BlockSpec(memory_space=pltpu.VMEM)
    dma = pltpu.SemaphoreType.DMA
    return pl.pallas_call(
        share_kernel,
        out_shape=jax.ShapeDtypeStruct((3, 32, ROWS * FACE), F32),
        in_specs=[vmem],
        out_specs=vmem,
        scratch_shapes=[pltpu.VMEM((4, 3, ROWS // 2, 32, PTS), F32), dma((4,)), dma((4,))],
        compiler_params=pltpu.CompilerParams(
            collective_id=1, has_side_effects=True, vmem_limit_bytes=32 << 20
        ),
    )(mine)


def body(slabs, partials, coords, neighbours, counts):
    lists = lax.pad(neighbours.T, jnp.int32(0), ((0, 24 - SLOTS, 0), (0, 0, 0)))
    lists = lists + lax.pad(counts[None], jnp.int32(0), ((16, 7, 0), (0, 0, 0)))
    tot, xyz, cnt, table, owner = gather(slabs, partials, coords, lists)
    mine = smooth(place, tot, xyz, cnt.reshape(-1), owner, table)
    return jnp.transpose(share(mine), (0, 2, 1))


def solution(mesh):
    placed = (P("events", None, "slab", None), P(None, "slab", None), P("slab", None), P("slab"))
    return jax.shard_map(
        functools.partial(body, mesh.shape["slab"]),
        mesh=mesh, in_specs=placed, out_specs=P(None, "slab", "events"), check_vma=False,
    )
```

```python
import functools
import math

import jax
import jax.numpy as jnp
from jax import lax
from jax.experimental import pallas as pl
from jax.experimental.pallas import tpu as pltpu
from jax.sharding import PartitionSpec as P

MESH = pl.DeviceIdType.MESH
F32 = jnp.float32
BF16 = jnp.bfloat16

FACE = 256
ROWS = 4
PTS = 128
COLS = 64
WIN = 80
SLOTS = 9
SIDE = 6.0
CHUNK = 256
UNROLL = 16
AHEAD = 8
MOST = (SLOTS * PTS + CHUNK - 1) // CHUNK
LINES = ROWS * COLS * MOST // PTS + 1
NULL = (ROWS + 2) * FACE
LOG2E = math.log2(math.e)
SCALE_XY = math.sqrt(LOG2E / 128.0)
SCALE_Z = math.sqrt(LOG2E / 8.0)
ROW_ORDER = (0, 3, 1, 2)
SHIFT = SLOTS
PLACE = SHIFT + SLOTS + 1
AFTER = PLACE + SLOTS + 1
WIDE = 32


def window(d):
    return pl.multiple_of(COLS * d - 8 + 8 * ((3 - d) // 3) - 8 * (d // 3), 8)


def swap(slab, index):
    return 2 * ((index // 2 + slab // 4) % 2) + index % 2


def place():
    slab = lax.axis_index("slab")
    return slab, swap(slab, lax.axis_index("events"))


def list_slots(slab, me, sizes, nbuf, tbuf, table, owner):
    lane = lax.broadcasted_iota(jnp.int32, (1, FACE), 1)
    near = []
    for row in range(-1, ROWS + 1):
        at = (row + ROWS) % ROWS * FACE
        line = sizes[(row + ROWS) // ROWS, 0:1, at : at + FACE]
        wide = jnp.broadcast_to(line, (8, FACE))
        near.append([pltpu.roll(wide, 1, 1)[:1], line, pltpu.roll(wide, FACE - 1, 1)[:1]])
    second_half = jnp.broadcast_to(me // 2, (SLOTS, PTS)) == 1
    odd = jnp.broadcast_to(me % 2, (SLOTS, PTS)) == 1
    left = lax.broadcasted_iota(jnp.int32, (SLOTS, PTS), 1) < COLS

    def own(upper, lower):
        upper = jnp.where(second_half, upper[:, PTS:], upper[:, :PTS])
        lower = jnp.where(second_half, lower[:, PTS:], lower[:, :PTS])
        upper = jnp.where(odd, pltpu.roll(upper, COLS, 1), upper)
        lower = jnp.where(odd, lower, pltpu.roll(lower, COLS, 1))
        return jnp.where(left, upper, lower)

    sources, lengths = [], []
    for row in range(ROWS):
        entry = nbuf[:SLOTS, row * FACE : (row + 1) * FACE]
        step = entry - (slab * (ROWS * FACE) + row * FACE + lane)
        used = jnp.zeros((SLOTS, FACE), jnp.int32)
        for i in range(3):
            for j in range(3):
                used = jnp.where(step == (i - 1) * FACE + j - 1, near[row + i][j], used)
        lengths.append(jnp.where(entry >= 0, used, 0))
        sources.append(jnp.where(entry >= 0, entry - (slab * (ROWS * FACE) - FACE), NULL))
    which = jnp.concatenate([own(*sources[:2]), own(*sources[2:])], axis=1)
    used = jnp.concatenate([own(*lengths[:2]), own(*lengths[2:])], axis=1)
    tbuf[0:SLOTS, :] = which * 8
    starts = [jnp.zeros((1, FACE), jnp.int32)]
    for slot in range(SLOTS):
        starts.append(starts[-1] + used[slot : slot + 1, :])
    chunks = jnp.broadcast_to((starts[-1] + (CHUNK - 1)) // CHUNK, (8, FACE))
    lanes = lax.broadcasted_iota(jnp.int32, (8, FACE), 1)
    ends = chunks
    for step in (1, 2, 4, 8, 16, 32, 64, 128):
        ends = ends + jnp.where(lanes >= step, pltpu.roll(ends, step, 1), 0)
    base = (ends - chunks)[:1]
    for slot in range(SLOTS + 1):
        tbuf[SHIFT + slot : SHIFT + slot + 1, :] = starts[slot] % PTS
        tbuf[PLACE + slot : PLACE + slot + 1, :] = (base * (CHUNK // PTS) + starts[slot] // PTS) * 8
    tbuf[AFTER : AFTER + 1, :] = ends[:1]
    item = lax.broadcasted_iota(jnp.int32, (8, PTS), 1)
    turned = jnp.concatenate(
        [jnp.broadcast_to(ends[:1, half * PTS : (half + 1) * PTS], (PTS, PTS)).T for half in range(2)],
        axis=0,
    )
    for line in range(LINES):
        passed = jnp.zeros((8, PTS), jnp.int32)
        for group in range(FACE // 8):
            passed = passed + (turned[group * 8 : group * 8 + 8] <= item + line * PTS).astype(jnp.int32)
        owner[line : line + 1, :] = jnp.sum(passed, axis=0, keepdims=True)
    for half in range(2):
        for k in range(AFTER + 1):
            table[k, half : half + 1, :] = tbuf[k : k + 1, half * PTS : (half + 1) * PTS]


def gather_kernel(
    slabs, parts, coords, lists, tot, xyz, cnt, table, owner,
    sizes, nbuf, tbuf, pbuf, loc, rx1, tx2, rx2, psem, lsem, s1, r1, s2, r2, hs, hr,
):
    slab, me = place()
    high, core = me // 2, me % 2
    event = lax.axis_index("events")
    mate = 2 * (event // 2) + (1 - core)
    across = 2 * (1 - event // 2) + core

    loads = []
    for i, row in enumerate(ROW_ORDER):
        load = pltpu.make_async_copy(
            parts.at[:, :, pl.ds(row * FACE, FACE), :], pbuf.at[row], psem.at[row]
        )
        load.start()
        loads.append(load)
    mine = window(me)
    local = [
        pltpu.make_async_copy(lists.at[16:24, :], sizes.at[1], lsem.at[ROWS]),
        pltpu.make_async_copy(lists.at[0:16, :], nbuf, lsem.at[ROWS + 1]),
    ]
    for row in range(ROWS):
        local.append(
            pltpu.make_async_copy(
                coords.at[:, pl.ds(row * FACE + mine, WIN), :], xyz.at[row + 1], lsem.at[row]
            )
        )
    for copy in local:
        copy.start()

    def beside(step):
        return {"slab": slab + step, "events": swap(slab + step, me)}

    barrier = pltpu.get_barrier_semaphore()
    for other in (mate, across):
        pl.semaphore_signal(barrier, inc=1, device_id={"events": other}, device_id_type=MESH)

    @pl.when(slab > 0)
    def _():
        pl.semaphore_signal(barrier, inc=1, device_id=beside(-1), device_id_type=MESH)

    @pl.when(slab < slabs - 1)
    def _():
        pl.semaphore_signal(barrier, inc=1, device_id=beside(1), device_id_type=MESH)

    pl.semaphore_wait(barrier, 4 - (slabs - 1 - slab) // (slabs - 1) - slab // (slabs - 1))

    def halo(up):
        row = 0 if up else ROWS - 1
        land = ROWS + 1 if up else 0
        side = 0 if up else 1
        pairs = (
            (coords.at[:, pl.ds(row * FACE + mine, WIN), :], xyz.at[land]),
            (lists.at[16:24, :], sizes.at[2 if up else 0]),
            (tot.at[row + 1], tot.at[land]),
        )
        return [
            pltpu.make_async_remote_copy(
                src_ref=src, dst_ref=dst, send_sem=hs.at[side, i], recv_sem=hr.at[side, i],
                device_id=beside(-1 if up else 1), device_id_type=MESH,
            )
            for i, (src, dst) in enumerate(pairs)
        ]

    ups, downs = halo(True), halo(False)

    @pl.when(slab > 0)
    def _():
        ups[1].start()
        ups[0].start()

    @pl.when(slab < slabs - 1)
    def _():
        downs[1].start()
        downs[0].start()

    first, second = {}, {}
    theirs = window(2 * (1 - high) + core)

    def cross(row):
        for half in range(2):
            first[row, half].wait_recv()
        tx2[row] = loc[row, :, pl.ds(theirs, WIN), :] + rx1[row, 1 - high]
        second[row] = pltpu.make_async_remote_copy(
            src_ref=tx2.at[row], dst_ref=rx2.at[row],
            send_sem=s2.at[row], recv_sem=r2.at[row],
            device_id={"events": across}, device_id_type=MESH,
        )
        second[row].start()

    for i, row in enumerate(ROW_ORDER):
        loads[i].wait()
        loc[row] = (pbuf[row, 0] + pbuf[row, 1]) + (pbuf[row, 2] + pbuf[row, 3])
        for half in range(2):
            first[row, half] = pltpu.make_async_remote_copy(
                src_ref=loc.at[row, :, pl.ds(window(2 * half + 1 - core), WIN), :],
                dst_ref=rx1.at[row, half],
                send_sem=s1.at[row, half], recv_sem=r1.at[row, half],
                device_id={"events": mate}, device_id_type=MESH,
            )
            first[row, half].start()
        if i > 0:
            cross(ROW_ORDER[i - 1])
    cross(ROW_ORDER[-1])
    for copy in local:
        copy.wait()

    @pl.when(slab > 0)
    def _():
        downs[1].wait_recv()

    @pl.when(slab < slabs - 1)
    def _():
        ups[1].wait_recv()

    @pl.when(slab == 0)
    def _():
        sizes[0] = jnp.zeros(sizes.shape[1:], jnp.int32)

    @pl.when(slab == slabs - 1)
    def _():
        sizes[2] = jnp.zeros(sizes.shape[1:], jnp.int32)

    for i in range(3):
        for j in range(8):
            cnt[i, j : j + 1, :] = sizes[i, 0:1, j * PTS : (j + 1) * PTS]
    list_slots(slab, me, sizes, nbuf, tbuf, table, owner)
    for row in ROW_ORDER:
        second[row].wait_recv()
        tot[row + 1] = (loc[row, :, pl.ds(mine, WIN), :] + rx1[row, high]) + rx2[row]
        if row == 0:

            @pl.when(slab > 0)
            def _():
                ups[2].start()

        if row == ROWS - 1:

            @pl.when(slab < slabs - 1)
            def _():
                downs[2].start()

    for row in ROW_ORDER:
        for half in range(2):
            first[row, half].wait_send()
        second[row].wait_send()

    @pl.when(slab > 0)
    def _():
        for copy in ups:
            copy.wait_send()
        downs[0].wait_recv()
        downs[2].wait_recv()

    @pl.when(slab < slabs - 1)
    def _():
        for copy in downs:
            copy.wait_send()
        ups[0].wait_recv()
        ups[2].wait_recv()

    @pl.when(slab == 0)
    def _():
        tot[0] = jnp.zeros(tot.shape[1:], F32)
        xyz[0] = jnp.zeros(xyz.shape[1:], F32)

    @pl.when(slab == slabs - 1)
    def _():
        tot[ROWS + 1] = jnp.zeros(tot.shape[1:], F32)
        xyz[ROWS + 1] = jnp.zeros(xyz.shape[1:], F32)


def gather(slabs, partials, coords, lists):
    vmem = pl.BlockSpec(memory_space=pltpu.VMEM)
    hbm = pl.BlockSpec(memory_space=pltpu.HBM)
    dma = pltpu.SemaphoreType.DMA
    return pl.pallas_call(
        functools.partial(gather_kernel, slabs),
        out_shape=(
            jax.ShapeDtypeStruct((ROWS + 2, 3, WIN, PTS), F32),
            jax.ShapeDtypeStruct((ROWS + 2, 3, WIN, PTS), F32),
            jax.ShapeDtypeStruct((3, 8, PTS), jnp.int32),
            jax.ShapeDtypeStruct((AFTER + 1, 8, PTS), jnp.int32),
            jax.ShapeDtypeStruct((LINES, PTS), jnp.int32),
        ),
        in_specs=[hbm, hbm, hbm],
        out_specs=(vmem, vmem, vmem, vmem, vmem),
        scratch_shapes=[
            pltpu.VMEM((3, 8, ROWS * FACE), jnp.int32),
            pltpu.VMEM((16, ROWS * FACE), jnp.int32),
            pltpu.VMEM((WIDE, FACE), jnp.int32),
            pltpu.VMEM((ROWS, 4, 3, FACE, PTS), F32),
            pltpu.VMEM((ROWS, 3, FACE, PTS), F32),
            pltpu.VMEM((ROWS, 2, 3, WIN, PTS), F32),
            pltpu.VMEM((ROWS, 3, WIN, PTS), F32),
            pltpu.VMEM((ROWS, 3, WIN, PTS), F32),
            dma((ROWS,)), dma((ROWS + 2,)),
            dma((ROWS, 2)), dma((ROWS, 2)), dma((ROWS,)), dma((ROWS,)),
            dma((2, 3)), dma((2, 3)),
        ],
        compiler_params=pltpu.CompilerParams(
            collective_id=0, has_side_effects=True, vmem_limit_bytes=52 << 20
        ),
    )(partials, coords, lists)


def split(values):
    high = values.astype(BF16)
    return high, (values - high.astype(F32)).astype(BF16)


def smooth_kernel(place, tot, xyz, cnts, owners, rows, out, src, centres, packed, acc, spread, held, staged, before, now, cnt, owner, sem, *table):
    slab, me = place()
    loads = [
        pltpu.make_async_copy(rows.at[k, 0:2, :], table[k], sem.at[k]) for k in range(AFTER + 1)
    ]
    first = pltpu.make_async_copy(cnts, cnt, sem.at[AFTER + 1])
    first.start()
    loads.append(pltpu.make_async_copy(owners, owner, sem.at[AFTER + 2]))
    for load in loads:
        load.start()
    start = window(me)
    lane = lax.broadcasted_iota(jnp.int32, (8, PTS), 1)
    sub = lax.broadcasted_iota(jnp.int32, (8, PTS), 0)
    zero = jnp.zeros((8, PTS), F32)

    def build(step, _):
        row = step // (WIN // 8)
        col = pl.multiple_of(step % (WIN // 8) * 8, 8)
        tile = row * FACE + start + col
        limit = jnp.zeros((8, PTS), jnp.int32)
        for i in range(8):
            limit = jnp.where(sub == i, cnt[tile + i + (ROWS - 1) * FACE], limit)
        valid = lane < limit
        for i in range(3):
            src[pl.ds(tile * 8 + i, 8, 8), :] = jnp.where(valid, tot[row, i, pl.ds(col, 8), :], 0.0)
            src[pl.ds(tile * 8 + 4 + i, 8, 8), :] = jnp.where(valid, xyz[row, i, pl.ds(col, 8), :], 0.0)
        src[pl.ds(tile * 8 + 3, 8, 8), :] = valid.astype(F32)
        src[pl.ds(tile * 8 + 7, 8, 8), :] = zero
        return 0

    src[NULL * 8 : NULL * 8 + 8, :] = zero

    def middle(step, _):
        row, col = step // (COLS // 8), step % (COLS // 8) * 8
        for i in range(8):
            value = zero
            if i == 4:
                value = zero + ((slab * ROWS + row).astype(F32) + 0.5) * SIDE
            if i == 5:
                value = ((sub + (me * COLS + col)).astype(F32) + 0.5) * SIDE
            if i == 6:
                value = zero + 0.5 * SIDE
            centres[pl.ds(step * 64 + i, 8, 8), :] = value
        return 0

    lax.fori_loop(0, ROWS * COLS // 8, middle, 0, unroll=4)
    centres[ROWS * COLS * 8 : ROWS * COLS * 8 + 8, :] = zero
    acc[...] = jnp.zeros_like(acc)
    first.wait()
    lax.fori_loop(0, (ROWS + 2) * (WIN // 8), build, 0, unroll=4)

    tiles = ROWS * COLS
    spare = tiles * MOST

    def look(k, tile):
        return table[k][tile >> 7, tile & (PTS - 1)]

    def pack(tile):
        for slot in range(SLOTS):
            shift = look(SHIFT + slot, tile)
            source = src[pl.ds(pl.multiple_of(look(slot, tile), 8), 8), :]
            turned = pltpu.roll(source, shift, 1)
            here = lane >= shift
            to = pl.multiple_of(look(PLACE + slot, tile), 8)
            pltpu.store(packed.at[pl.ds(to, 8), :], turned, mask=here)
            pltpu.store(packed.at[pl.ds(to + 8, 8), :], turned, mask=jnp.logical_not(here))
        to = pl.multiple_of(look(PLACE + SLOTS, tile), 8)
        pltpu.store(packed.at[pl.ds(to, 8), :], zero, mask=lane >= look(SHIFT + SLOTS, tile))
        packed[pl.ds(to + 8, 8), :] = zero

    packed[spare * 16 : spare * 16 + 8, :] = zero
    packed[spare * 16 + 8 : spare * 16 + 16, :] = zero
    for load in loads:
        load.wait()
    scale = jnp.where(sub < 4, 1.0, jnp.where(sub < 6, SCALE_XY, SCALE_Z)).astype(F32)
    scale2 = jnp.where(sub < 4, 0.0, jnp.where(sub < 6, 2.0 * SCALE_XY, 2.0 * SCALE_Z)).astype(F32)
    minus = jnp.where((sub >= 4) & (sub < 7), -1.0, 0.0).astype(F32)
    minus = jnp.concatenate([minus, minus], axis=0).astype(BF16)

    def item(i):
        tile = now[i]
        centre = centres[pl.ds(pl.multiple_of(tile * 8, 8), 8), :]
        boths, squares = [], []
        for half in range(CHUNK // PTS):
            points = (staged[i, half * 8 : half * 8 + 8, :] - centre) * scale
            boths.append(jnp.concatenate(split(points), axis=0))
            squares.append(jnp.concatenate(split(points * points), axis=0))
        both = jnp.concatenate(boths, axis=1)
        sources = jnp.concatenate([both, both, jnp.concatenate(squares, axis=1)], axis=0)
        index = pl.multiple_of(((tile >> 6) * FACE + (tile & 63) + (FACE + me * COLS)) * 8, 8)
        query = (src[pl.ds(index, 8), :] - centre) * scale2
        q_high, q_low = split(query)
        queries = jnp.concatenate([q_high, q_high, q_low, q_low, minus], axis=0)
        return tile, both, sources, queries

    def advance(taken, made, beside):
        for i in range(UNROLL):
            at = jnp.where(taken + i < made, taken + i, spare)
            staged[i] = packed[pl.ds(pl.multiple_of(at * 16, 16), 16), :]
            now[i] = owner[at >> 7, at & (PTS - 1)]
        todo = [item(i) for i in range(UNROLL)]
        for i in range(UNROLL):
            tile, both, sources, queries = todo[i]
            high, low = split(jnp.exp2(spread[i]))
            got = jnp.dot(held[i], jnp.concatenate([high, low], axis=1), preferred_element_type=F32)
            got = got[:, :PTS] + got[:, PTS:]
            at = pl.ds(pl.multiple_of(before[i] * 8, 8), 8)
            acc[at, :] = acc[at, :] + (got[:8] + got[8:])
            spread[i] = lax.dot_general(
                sources, queries, (((0,), (0,)), ((), ())), preferred_element_type=F32
            )
            held[i] = both
            before[i] = tile
            beside(i)
        return jnp.minimum(taken + UNROLL, made)

    for i in range(UNROLL):
        before[i] = tiles

    def fused(step, carry):
        made, taken = carry

        def beside(i):
            if i % (UNROLL // AHEAD) == 0:
                pack(step * AHEAD + i // (UNROLL // AHEAD))

        taken = advance(taken, made, beside)
        return look(AFTER, (step + 1) * AHEAD - 1), taken

    made, taken = lax.fori_loop(0, tiles // AHEAD, fused, (0, 0))
    steps = (made - taken + UNROLL - 1) // UNROLL + 1
    lax.fori_loop(0, steps, lambda _, t: advance(t, made, lambda i: None), taken)

    for pair in range(ROWS // 2):
        top = pair * 2 * COLS * 8
        flags = [
            src[pl.ds(((2 * pair + i + 1) * FACE + me * COLS) * 8 + 3, COLS, 8), :] for i in range(2)
        ]
        valid = jnp.concatenate(flags, axis=0) > 0.0
        share = 1.0 / jnp.where(valid, acc[pl.ds(top + 3, 2 * COLS, 8), :], 1.0)
        for k in range(3):
            value = jnp.where(valid, acc[pl.ds(top + k, 2 * COLS, 8), :] * share, 0.0).T
            for d in range(4):
                out[d, k, pair] = value[d * 32 : d * 32 + 32]


def smooth(place, tot, xyz, cnt, owner, table):
    vmem = pl.BlockSpec(memory_space=pltpu.VMEM)
    tiles = ROWS * COLS
    most = tiles * MOST + 1
    return pl.pallas_call(
        functools.partial(smooth_kernel, place),
        out_shape=jax.ShapeDtypeStruct((4, 3, ROWS // 2, 32, PTS), F32),
        in_specs=[vmem, vmem, vmem, vmem, vmem],
        out_specs=vmem,
        scratch_shapes=[
            pltpu.VMEM(((NULL + 1) * 8, PTS), F32),
            pltpu.VMEM(((tiles + 1) * 8, PTS), F32),
            pltpu.VMEM((most * 16, PTS), F32),
            pltpu.VMEM(((tiles + 1) * 8, PTS), F32),
            pltpu.VMEM((UNROLL, CHUNK, PTS), F32),
            pltpu.VMEM((UNROLL, 16, CHUNK), BF16),
            pltpu.VMEM((UNROLL, 16, PTS), F32),
            pltpu.SMEM((UNROLL,), jnp.int32),
            pltpu.SMEM((UNROLL,), jnp.int32),
            pltpu.SMEM((3 * ROWS * FACE,), jnp.int32),
            pltpu.SMEM((LINES, PTS), jnp.int32),
            pltpu.SemaphoreType.DMA((AFTER + 3,)),
            *[pltpu.SMEM((2, PTS), jnp.int32)] * (AFTER + 1),
        ],
        compiler_params=pltpu.CompilerParams(vmem_limit_bytes=48 << 20),
    )(tot, xyz, cnt, owner, table)


def share_kernel(mine, out, rx, ssem, rsem):
    slab, block = place()
    me = lax.axis_index("events")
    barrier = pltpu.get_barrier_semaphore()
    for i in range(1, 4):
        pl.semaphore_signal(barrier, inc=1, device_id={"events": (me + i) % 4}, device_id_type=MESH)
    pl.semaphore_wait(barrier, 3)

    def copy(target, slot):
        return pltpu.make_async_remote_copy(
            src_ref=mine.at[target], dst_ref=rx.at[slot],
            send_sem=ssem.at[target], recv_sem=rsem.at[slot],
            device_id={"events": target}, device_id_type=MESH,
        )

    for i in (2, 3, 1):
        copy((me + i) % 4, block).start()
    rx[block] = mine[me]
    for i in (1, 3, 2):
        other = (me + i) % 4
        copy(other, swap(slab, other)).wait_recv()
    left = lax.broadcasted_iota(jnp.int32, (32, PTS), 1) < COLS
    for k in range(3):
        for pair in range(ROWS // 2):
            for half in range(2):
                a, b = rx[2 * half, k, pair], rx[2 * half + 1, k, pair]
                upper = 2 * pair * FACE + half * PTS
                lower = upper + FACE
                out[k, :, upper : upper + PTS] = jnp.where(left, a, pltpu.roll(b, COLS, 1))
                out[k, :, lower : lower + PTS] = jnp.where(left, pltpu.roll(a, COLS, 1), b)
    for i in range(1, 4):
        copy((me + i) % 4, block).wait_send()


def share(mine):
    vmem = pl.BlockSpec(memory_space=pltpu.VMEM)
    dma = pltpu.SemaphoreType.DMA
    return pl.pallas_call(
        share_kernel,
        out_shape=jax.ShapeDtypeStruct((3, 32, ROWS * FACE), F32),
        in_specs=[vmem],
        out_specs=vmem,
        scratch_shapes=[pltpu.VMEM((4, 3, ROWS // 2, 32, PTS), F32), dma((4,)), dma((4,))],
        compiler_params=pltpu.CompilerParams(
            collective_id=1, has_side_effects=True, vmem_limit_bytes=32 << 20
        ),
    )(mine)


def body(slabs, partials, coords, neighbours, counts):
    lists = lax.pad(neighbours.T, jnp.int32(0), ((0, 24 - SLOTS, 0), (0, 0, 0)))
    lists = lists + lax.pad(counts[None], jnp.int32(0), ((16, 7, 0), (0, 0, 0)))
    tot, xyz, cnt, table, owner = gather(slabs, partials, coords, lists)
    mine = smooth(place, tot, xyz, cnt.reshape(-1), owner, table)
    return jnp.transpose(share(mine), (0, 2, 1))


def solution(mesh):
    placed = (P("events", None, "slab", None), P(None, "slab", None), P("slab", None), P("slab"))
    return jax.shard_map(
        functools.partial(body, mesh.shape["slab"]),
        mesh=mesh, in_specs=placed, out_specs=P(None, "slab", "events"), check_vma=False,
    )
```

```python
import functools
import math

import jax
import jax.numpy as jnp
from jax import lax
from jax.experimental import pallas as pl
from jax.experimental.pallas import tpu as pltpu
from jax.sharding import PartitionSpec as P

MESH = pl.DeviceIdType.MESH
F32 = jnp.float32
BF16 = jnp.bfloat16

FACE = 256
ROWS = 4
PTS = 128
COLS = 64
WIN = 80
SLOTS = 9
SIDE = 6.0
CHUNK = 256
UNROLL = 16
AHEAD = 8
MOST = (SLOTS * PTS + CHUNK - 1) // CHUNK
LINES = ROWS * COLS * MOST // PTS + 1
NULL = (ROWS + 2) * FACE
LOG2E = math.log2(math.e)
SCALE_XY = math.sqrt(LOG2E / 128.0)
SCALE_Z = math.sqrt(LOG2E / 8.0)
ROW_ORDER = (0, 3, 1, 2)
SHIFT = SLOTS
PLACE = SHIFT + SLOTS + 1
AFTER = PLACE + SLOTS + 1
WIDE = 32


def window(d):
    return pl.multiple_of(COLS * d - 8 + 8 * ((3 - d) // 3) - 8 * (d // 3), 8)


def swap(slab, index):
    return 2 * ((index // 2 + slab // 4) % 2) + index % 2


def place():
    slab = lax.axis_index("slab")
    return slab, swap(slab, lax.axis_index("events"))


def list_slots(slab, me, sizes, nbuf, tbuf, table, owner):
    lane = lax.broadcasted_iota(jnp.int32, (1, FACE), 1)
    near = []
    for row in range(-1, ROWS + 1):
        at = (row + ROWS) % ROWS * FACE
        line = sizes[(row + ROWS) // ROWS, 0:1, at : at + FACE]
        wide = jnp.broadcast_to(line, (8, FACE))
        near.append([pltpu.roll(wide, 1, 1)[:1], line, pltpu.roll(wide, FACE - 1, 1)[:1]])
    second_half = jnp.broadcast_to(me // 2, (SLOTS, PTS)) == 1
    odd = jnp.broadcast_to(me % 2, (SLOTS, PTS)) == 1
    left = lax.broadcasted_iota(jnp.int32, (SLOTS, PTS), 1) < COLS

    def own(upper, lower):
        upper = jnp.where(second_half, upper[:, PTS:], upper[:, :PTS])
        lower = jnp.where(second_half, lower[:, PTS:], lower[:, :PTS])
        upper = jnp.where(odd, pltpu.roll(upper, COLS, 1), upper)
        lower = jnp.where(odd, lower, pltpu.roll(lower, COLS, 1))
        return jnp.where(left, upper, lower)

    sources, lengths = [], []
    for row in range(ROWS):
        entry = nbuf[:SLOTS, row * FACE : (row + 1) * FACE]
        step = entry - (slab * (ROWS * FACE) + row * FACE + lane)
        used = jnp.zeros((SLOTS, FACE), jnp.int32)
        for i in range(3):
            for j in range(3):
                used = jnp.where(step == (i - 1) * FACE + j - 1, near[row + i][j], used)
        lengths.append(jnp.where(entry >= 0, used, 0))
        sources.append(jnp.where(entry >= 0, entry - (slab * (ROWS * FACE) - FACE), NULL))
    which = jnp.concatenate([own(*sources[:2]), own(*sources[2:])], axis=1)
    used = jnp.concatenate([own(*lengths[:2]), own(*lengths[2:])], axis=1)
    tbuf[0:SLOTS, :] = which * 8
    starts = [jnp.zeros((1, FACE), jnp.int32)]
    for slot in range(SLOTS):
        starts.append(starts[-1] + used[slot : slot + 1, :])
    chunks = jnp.broadcast_to((starts[-1] + (CHUNK - 1)) // CHUNK, (8, FACE))
    lanes = lax.broadcasted_iota(jnp.int32, (8, FACE), 1)
    ends = chunks
    for step in (1, 2, 4, 8, 16, 32, 64, 128):
        ends = ends + jnp.where(lanes >= step, pltpu.roll(ends, step, 1), 0)
    base = (ends - chunks)[:1]
    for slot in range(SLOTS + 1):
        tbuf[SHIFT + slot : SHIFT + slot + 1, :] = starts[slot] % PTS
        tbuf[PLACE + slot : PLACE + slot + 1, :] = (base * (CHUNK // PTS) + starts[slot] // PTS) * 8
    tbuf[AFTER : AFTER + 1, :] = ends[:1]
    item = lax.broadcasted_iota(jnp.int32, (8, PTS), 1)
    turned = jnp.concatenate(
        [jnp.broadcast_to(ends[:1, half * PTS : (half + 1) * PTS], (PTS, PTS)).T for half in range(2)],
        axis=0,
    )
    for line in range(LINES):
        passed = jnp.zeros((8, PTS), jnp.int32)
        for group in range(FACE // 8):
            passed = passed + (turned[group * 8 : group * 8 + 8] <= item + line * PTS).astype(jnp.int32)
        owner[line : line + 1, :] = jnp.sum(passed, axis=0, keepdims=True)
    for half in range(2):
        for k in range(AFTER + 1):
            table[k, half : half + 1, :] = tbuf[k : k + 1, half * PTS : (half + 1) * PTS]


def gather_kernel(
    slabs, parts, coords, lists, tot, xyz, cnt, table, owner,
    sizes, nbuf, tbuf, pbuf, loc, rx1, tx2, rx2, psem, lsem, s1, r1, s2, r2, hs, hr,
):
    slab, me = place()
    high, core = me // 2, me % 2
    event = lax.axis_index("events")
    mate = 2 * (event // 2) + (1 - core)
    across = 2 * (1 - event // 2) + core

    loads = []
    for i, row in enumerate(ROW_ORDER):
        load = pltpu.make_async_copy(
            parts.at[:, :, pl.ds(row * FACE, FACE), :], pbuf.at[row], psem.at[row]
        )
        load.start()
        loads.append(load)
    mine = window(me)
    local = [
        pltpu.make_async_copy(lists.at[16:24, :], sizes.at[1], lsem.at[ROWS]),
        pltpu.make_async_copy(lists.at[0:16, :], nbuf, lsem.at[ROWS + 1]),
    ]
    for row in range(ROWS):
        local.append(
            pltpu.make_async_copy(
                coords.at[:, pl.ds(row * FACE + mine, WIN), :], xyz.at[row + 1], lsem.at[row]
            )
        )
    for copy in local:
        copy.start()

    def beside(step):
        return {"slab": slab + step, "events": swap(slab + step, me)}

    barrier = pltpu.get_barrier_semaphore()
    for other in (mate, across):
        pl.semaphore_signal(barrier, inc=1, device_id={"events": other}, device_id_type=MESH)

    @pl.when(slab > 0)
    def _():
        pl.semaphore_signal(barrier, inc=1, device_id=beside(-1), device_id_type=MESH)

    @pl.when(slab < slabs - 1)
    def _():
        pl.semaphore_signal(barrier, inc=1, device_id=beside(1), device_id_type=MESH)

    pl.semaphore_wait(barrier, 4 - (slabs - 1 - slab) // (slabs - 1) - slab // (slabs - 1))

    def halo(up):
        row = 0 if up else ROWS - 1
        land = ROWS + 1 if up else 0
        side = 0 if up else 1
        pairs = (
            (coords.at[:, pl.ds(row * FACE + mine, WIN), :], xyz.at[land]),
            (lists.at[16:24, :], sizes.at[2 if up else 0]),
            (tot.at[row + 1], tot.at[land]),
        )
        return [
            pltpu.make_async_remote_copy(
                src_ref=src, dst_ref=dst, send_sem=hs.at[side, i], recv_sem=hr.at[side, i],
                device_id=beside(-1 if up else 1), device_id_type=MESH,
            )
            for i, (src, dst) in enumerate(pairs)
        ]

    ups, downs = halo(True), halo(False)

    @pl.when(slab > 0)
    def _():
        ups[1].start()
        ups[0].start()

    @pl.when(slab < slabs - 1)
    def _():
        downs[1].start()
        downs[0].start()

    first, second = {}, {}
    theirs = window(2 * (1 - high) + core)

    def cross(row):
        for half in range(2):
            first[row, half].wait_recv()
        tx2[row] = loc[row, :, pl.ds(theirs, WIN), :] + rx1[row, 1 - high]
        second[row] = pltpu.make_async_remote_copy(
            src_ref=tx2.at[row], dst_ref=rx2.at[row],
            send_sem=s2.at[row], recv_sem=r2.at[row],
            device_id={"events": across}, device_id_type=MESH,
        )
        second[row].start()

    for i, row in enumerate(ROW_ORDER):
        loads[i].wait()
        loc[row] = (pbuf[row, 0] + pbuf[row, 1]) + (pbuf[row, 2] + pbuf[row, 3])
        for half in range(2):
            first[row, half] = pltpu.make_async_remote_copy(
                src_ref=loc.at[row, :, pl.ds(window(2 * half + 1 - core), WIN), :],
                dst_ref=rx1.at[row, half],
                send_sem=s1.at[row, half], recv_sem=r1.at[row, half],
                device_id={"events": mate}, device_id_type=MESH,
            )
            first[row, half].start()
        if i > 0:
            cross(ROW_ORDER[i - 1])
    cross(ROW_ORDER[-1])
    for row in ROW_ORDER[:2]:
        second[row].wait_recv()
        tot[row + 1] = (loc[row, :, pl.ds(mine, WIN), :] + rx1[row, high]) + rx2[row]
        if row == 0:

            @pl.when(slab > 0)
            def _():
                ups[2].start()

        if row == ROWS - 1:

            @pl.when(slab < slabs - 1)
            def _():
                downs[2].start()

    for copy in local:
        copy.wait()

    @pl.when(slab > 0)
    def _():
        downs[1].wait_recv()

    @pl.when(slab < slabs - 1)
    def _():
        ups[1].wait_recv()

    @pl.when(slab == 0)
    def _():
        sizes[0] = jnp.zeros(sizes.shape[1:], jnp.int32)

    @pl.when(slab == slabs - 1)
    def _():
        sizes[2] = jnp.zeros(sizes.shape[1:], jnp.int32)

    for i in range(3):
        for j in range(8):
            cnt[i, j : j + 1, :] = sizes[i, 0:1, j * PTS : (j + 1) * PTS]
    list_slots(slab, me, sizes, nbuf, tbuf, table, owner)
    for row in ROW_ORDER[2:]:
        second[row].wait_recv()
        tot[row + 1] = (loc[row, :, pl.ds(mine, WIN), :] + rx1[row, high]) + rx2[row]

    for row in ROW_ORDER:
        for half in range(2):
            first[row, half].wait_send()
        second[row].wait_send()

    @pl.when(slab > 0)
    def _():
        for copy in ups:
            copy.wait_send()
        downs[0].wait_recv()
        downs[2].wait_recv()

    @pl.when(slab < slabs - 1)
    def _():
        for copy in downs:
            copy.wait_send()
        ups[0].wait_recv()
        ups[2].wait_recv()

    @pl.when(slab == 0)
    def _():
        tot[0] = jnp.zeros(tot.shape[1:], F32)
        xyz[0] = jnp.zeros(xyz.shape[1:], F32)

    @pl.when(slab == slabs - 1)
    def _():
        tot[ROWS + 1] = jnp.zeros(tot.shape[1:], F32)
        xyz[ROWS + 1] = jnp.zeros(xyz.shape[1:], F32)


def gather(slabs, partials, coords, lists):
    vmem = pl.BlockSpec(memory_space=pltpu.VMEM)
    hbm = pl.BlockSpec(memory_space=pltpu.HBM)
    dma = pltpu.SemaphoreType.DMA
    return pl.pallas_call(
        functools.partial(gather_kernel, slabs),
        out_shape=(
            jax.ShapeDtypeStruct((ROWS + 2, 3, WIN, PTS), F32),
            jax.ShapeDtypeStruct((ROWS + 2, 3, WIN, PTS), F32),
            jax.ShapeDtypeStruct((3, 8, PTS), jnp.int32),
            jax.ShapeDtypeStruct((AFTER + 1, 8, PTS), jnp.int32),
            jax.ShapeDtypeStruct((LINES, PTS), jnp.int32),
        ),
        in_specs=[hbm, hbm, hbm],
        out_specs=(vmem, vmem, vmem, vmem, vmem),
        scratch_shapes=[
            pltpu.VMEM((3, 8, ROWS * FACE), jnp.int32),
            pltpu.VMEM((16, ROWS * FACE), jnp.int32),
            pltpu.VMEM((WIDE, FACE), jnp.int32),
            pltpu.VMEM((ROWS, 4, 3, FACE, PTS), F32),
            pltpu.VMEM((ROWS, 3, FACE, PTS), F32),
            pltpu.VMEM((ROWS, 2, 3, WIN, PTS), F32),
            pltpu.VMEM((ROWS, 3, WIN, PTS), F32),
            pltpu.VMEM((ROWS, 3, WIN, PTS), F32),
            dma((ROWS,)), dma((ROWS + 2,)),
            dma((ROWS, 2)), dma((ROWS, 2)), dma((ROWS,)), dma((ROWS,)),
            dma((2, 3)), dma((2, 3)),
        ],
        compiler_params=pltpu.CompilerParams(
            collective_id=0, has_side_effects=True, vmem_limit_bytes=52 << 20
        ),
    )(partials, coords, lists)


def split(values):
    high = values.astype(BF16)
    return high, (values - high.astype(F32)).astype(BF16)


def smooth_kernel(place, tot, xyz, cnts, owners, rows, out, src, centres, packed, acc, spread, held, staged, before, now, cnt, owner, sem, *table):
    slab, me = place()
    loads = [
        pltpu.make_async_copy(rows.at[k, 0:2, :], table[k], sem.at[k]) for k in range(AFTER + 1)
    ]
    first = pltpu.make_async_copy(cnts, cnt, sem.at[AFTER + 1])
    first.start()
    loads.append(pltpu.make_async_copy(owners, owner, sem.at[AFTER + 2]))
    for load in loads:
        load.start()
    start = window(me)
    lane = lax.broadcasted_iota(jnp.int32, (8, PTS), 1)
    sub = lax.broadcasted_iota(jnp.int32, (8, PTS), 0)
    zero = jnp.zeros((8, PTS), F32)

    def build(step, _):
        row = step // (WIN // 8)
        col = pl.multiple_of(step % (WIN // 8) * 8, 8)
        tile = row * FACE + start + col
        limit = jnp.zeros((8, PTS), jnp.int32)
        for i in range(8):
            limit = jnp.where(sub == i, cnt[tile + i + (ROWS - 1) * FACE], limit)
        valid = lane < limit
        for i in range(3):
            src[pl.ds(tile * 8 + i, 8, 8), :] = jnp.where(valid, tot[row, i, pl.ds(col, 8), :], 0.0)
            src[pl.ds(tile * 8 + 4 + i, 8, 8), :] = jnp.where(valid, xyz[row, i, pl.ds(col, 8), :], 0.0)
        src[pl.ds(tile * 8 + 3, 8, 8), :] = valid.astype(F32)
        src[pl.ds(tile * 8 + 7, 8, 8), :] = zero
        return 0

    src[NULL * 8 : NULL * 8 + 8, :] = zero

    def middle(step, _):
        row, col = step // (COLS // 8), step % (COLS // 8) * 8
        for i in range(8):
            value = zero
            if i == 4:
                value = zero + ((slab * ROWS + row).astype(F32) + 0.5) * SIDE
            if i == 5:
                value = ((sub + (me * COLS + col)).astype(F32) + 0.5) * SIDE
            if i == 6:
                value = zero + 0.5 * SIDE
            centres[pl.ds(step * 64 + i, 8, 8), :] = value
        return 0

    lax.fori_loop(0, ROWS * COLS // 8, middle, 0, unroll=4)
    centres[ROWS * COLS * 8 : ROWS * COLS * 8 + 8, :] = zero
    acc[...] = jnp.zeros_like(acc)
    first.wait()
    lax.fori_loop(0, (ROWS + 2) * (WIN // 8), build, 0, unroll=4)

    tiles = ROWS * COLS
    spare = tiles * MOST

    def look(k, tile):
        return table[k][tile >> 7, tile & (PTS - 1)]

    def pack(tile):
        for slot in range(SLOTS):
            shift = look(SHIFT + slot, tile)
            source = src[pl.ds(pl.multiple_of(look(slot, tile), 8), 8), :]
            turned = pltpu.roll(source, shift, 1)
            here = lane >= shift
            to = pl.multiple_of(look(PLACE + slot, tile), 8)
            pltpu.store(packed.at[pl.ds(to, 8), :], turned, mask=here)
            pltpu.store(packed.at[pl.ds(to + 8, 8), :], turned, mask=jnp.logical_not(here))
        to = pl.multiple_of(look(PLACE + SLOTS, tile), 8)
        pltpu.store(packed.at[pl.ds(to, 8), :], zero, mask=lane >= look(SHIFT + SLOTS, tile))
        packed[pl.ds(to + 8, 8), :] = zero

    packed[spare * 16 : spare * 16 + 8, :] = zero
    packed[spare * 16 + 8 : spare * 16 + 16, :] = zero
    for load in loads:
        load.wait()
    scale = jnp.where(sub < 4, 1.0, jnp.where(sub < 6, SCALE_XY, SCALE_Z)).astype(F32)
    scale2 = jnp.where(sub < 4, 0.0, jnp.where(sub < 6, 2.0 * SCALE_XY, 2.0 * SCALE_Z)).astype(F32)
    minus = jnp.where((sub >= 4) & (sub < 7), -1.0, 0.0).astype(F32)
    minus = jnp.concatenate([minus, minus], axis=0).astype(BF16)

    def item(i):
        tile = now[i]
        centre = centres[pl.ds(pl.multiple_of(tile * 8, 8), 8), :]
        boths, squares = [], []
        for half in range(CHUNK // PTS):
            points = (staged[i, half * 8 : half * 8 + 8, :] - centre) * scale
            boths.append(jnp.concatenate(split(points), axis=0))
            squares.append(jnp.concatenate(split(points * points), axis=0))
        both = jnp.concatenate(boths, axis=1)
        sources = jnp.concatenate([both, both, jnp.concatenate(squares, axis=1)], axis=0)
        index = pl.multiple_of(((tile >> 6) * FACE + (tile & 63) + (FACE + me * COLS)) * 8, 8)
        query = (src[pl.ds(index, 8), :] - centre) * scale2
        q_high, q_low = split(query)
        queries = jnp.concatenate([q_high, q_high, q_low, q_low, minus], axis=0)
        return tile, both, sources, queries

    def advance(taken, made, beside):
        for i in range(UNROLL):
            at = jnp.where(taken + i < made, taken + i, spare)
            staged[i] = packed[pl.ds(pl.multiple_of(at * 16, 16), 16), :]
            now[i] = owner[at >> 7, at & (PTS - 1)]
        todo = [item(i) for i in range(UNROLL)]
        for i in range(UNROLL):
            tile, both, sources, queries = todo[i]
            high, low = split(jnp.exp2(spread[i]))
            got = jnp.dot(held[i], jnp.concatenate([high, low], axis=1), preferred_element_type=F32)
            got = got[:, :PTS] + got[:, PTS:]
            at = pl.ds(pl.multiple_of(before[i] * 8, 8), 8)
            acc[at, :] = acc[at, :] + (got[:8] + got[8:])
            spread[i] = lax.dot_general(
                sources, queries, (((0,), (0,)), ((), ())), preferred_element_type=F32
            )
            held[i] = both
            before[i] = tile
            beside(i)
        return jnp.minimum(taken + UNROLL, made)

    for i in range(UNROLL):
        before[i] = tiles

    def fused(step, carry):
        made, taken = carry

        def beside(i):
            if i % (UNROLL // AHEAD) == 0:
                pack(step * AHEAD + i // (UNROLL // AHEAD))

        taken = advance(taken, made, beside)
        return look(AFTER, (step + 1) * AHEAD - 1), taken

    made, taken = lax.fori_loop(0, tiles // AHEAD, fused, (0, 0))
    steps = (made - taken + UNROLL - 1) // UNROLL + 1
    lax.fori_loop(0, steps, lambda _, t: advance(t, made, lambda i: None), taken)

    for pair in range(ROWS // 2):
        top = pair * 2 * COLS * 8
        flags = [
            src[pl.ds(((2 * pair + i + 1) * FACE + me * COLS) * 8 + 3, COLS, 8), :] for i in range(2)
        ]
        valid = jnp.concatenate(flags, axis=0) > 0.0
        share = 1.0 / jnp.where(valid, acc[pl.ds(top + 3, 2 * COLS, 8), :], 1.0)
        for k in range(3):
            value = jnp.where(valid, acc[pl.ds(top + k, 2 * COLS, 8), :] * share, 0.0).T
            for d in range(4):
                out[d, k, pair] = value[d * 32 : d * 32 + 32]


def smooth(place, tot, xyz, cnt, owner, table):
    vmem = pl.BlockSpec(memory_space=pltpu.VMEM)
    tiles = ROWS * COLS
    most = tiles * MOST + 1
    return pl.pallas_call(
        functools.partial(smooth_kernel, place),
        out_shape=jax.ShapeDtypeStruct((4, 3, ROWS // 2, 32, PTS), F32),
        in_specs=[vmem, vmem, vmem, vmem, vmem],
        out_specs=vmem,
        scratch_shapes=[
            pltpu.VMEM(((NULL + 1) * 8, PTS), F32),
            pltpu.VMEM(((tiles + 1) * 8, PTS), F32),
            pltpu.VMEM((most * 16, PTS), F32),
            pltpu.VMEM(((tiles + 1) * 8, PTS), F32),
            pltpu.VMEM((UNROLL, CHUNK, PTS), F32),
            pltpu.VMEM((UNROLL, 16, CHUNK), BF16),
            pltpu.VMEM((UNROLL, 16, PTS), F32),
            pltpu.SMEM((UNROLL,), jnp.int32),
            pltpu.SMEM((UNROLL,), jnp.int32),
            pltpu.SMEM((3 * ROWS * FACE,), jnp.int32),
            pltpu.SMEM((LINES, PTS), jnp.int32),
            pltpu.SemaphoreType.DMA((AFTER + 3,)),
            *[pltpu.SMEM((2, PTS), jnp.int32)] * (AFTER + 1),
        ],
        compiler_params=pltpu.CompilerParams(vmem_limit_bytes=48 << 20),
    )(tot, xyz, cnt, owner, table)


def share_kernel(mine, out, rx, ssem, rsem):
    slab, block = place()
    me = lax.axis_index("events")
    barrier = pltpu.get_barrier_semaphore()
    for i in range(1, 4):
        pl.semaphore_signal(barrier, inc=1, device_id={"events": (me + i) % 4}, device_id_type=MESH)
    pl.semaphore_wait(barrier, 3)

    def copy(target, slot):
        return pltpu.make_async_remote_copy(
            src_ref=mine.at[target], dst_ref=rx.at[slot],
            send_sem=ssem.at[target], recv_sem=rsem.at[slot],
            device_id={"events": target}, device_id_type=MESH,
        )

    for i in (2, 3, 1):
        copy((me + i) % 4, block).start()
    rx[block] = mine[me]
    for i in (1, 3, 2):
        other = (me + i) % 4
        copy(other, swap(slab, other)).wait_recv()
    left = lax.broadcasted_iota(jnp.int32, (32, PTS), 1) < COLS
    for k in range(3):
        for pair in range(ROWS // 2):
            for half in range(2):
                a, b = rx[2 * half, k, pair], rx[2 * half + 1, k, pair]
                upper = 2 * pair * FACE + half * PTS
                lower = upper + FACE
                out[k, :, upper : upper + PTS] = jnp.where(left, a, pltpu.roll(b, COLS, 1))
                out[k, :, lower : lower + PTS] = jnp.where(left, pltpu.roll(a, COLS, 1), b)
    for i in range(1, 4):
        copy((me + i) % 4, block).wait_send()


def share(mine):
    vmem = pl.BlockSpec(memory_space=pltpu.VMEM)
    dma = pltpu.SemaphoreType.DMA
    return pl.pallas_call(
        share_kernel,
        out_shape=jax.ShapeDtypeStruct((3, 32, ROWS * FACE), F32),
        in_specs=[vmem],
        out_specs=vmem,
        scratch_shapes=[pltpu.VMEM((4, 3, ROWS // 2, 32, PTS), F32), dma((4,)), dma((4,))],
        compiler_params=pltpu.CompilerParams(
            collective_id=1, has_side_effects=True, vmem_limit_bytes=32 << 20
        ),
    )(mine)


def body(slabs, partials, coords, neighbours, counts):
    lists = lax.pad(neighbours.T, jnp.int32(0), ((0, 24 - SLOTS, 0), (0, 0, 0)))
    lists = lists + lax.pad(counts[None], jnp.int32(0), ((16, 7, 0), (0, 0, 0)))
    tot, xyz, cnt, table, owner = gather(slabs, partials, coords, lists)
    mine = smooth(place, tot, xyz, cnt.reshape(-1), owner, table)
    return jnp.transpose(share(mine), (0, 2, 1))


def solution(mesh):
    placed = (P("events", None, "slab", None), P(None, "slab", None), P("slab", None), P("slab"))
    return jax.shard_map(
        functools.partial(body, mesh.shape["slab"]),
        mesh=mesh, in_specs=placed, out_specs=P(None, "slab", "events"), check_vma=False,
    )
```
